512 devices in a mesh: row: 32 (over x, y), col: 16 (over z, core).
Axes of the slice: x: 4, y: 8, z: 8, core: 2. Of those that a mesh axis runs over, the one named last changes fastest.
Arguments:
- right_side: bfloat16 [5, 8, 512, 2048], P(None, None, 'row', 'col'), as said below
- near_bands: bfloat16 [3, 2, 8, 512, 2048], P(None, None, None, 'row', 'col'), as said below
- margins: bfloat16 [3, 8, 512, 2048], P(None, None, 'row', 'col'), as said below
Outputs:
- update: float32 [5, 8, 512, 2048], P(None, None, 'row', 'col')
Inputs may be any that keep to these rules, and one draw needn't show every extreme that they name: `right_side`: every entry has magnitude at most 2 (2048)^(-3/2). `near_bands`: every entry lies between -0.9 and -0.2. `margins`: every entry is positive and at most 2.
All inputs are finite; a program needn't handle non-finite values.
Results may differ from the reference program's by a relative error of at most 0.005.
Values sent between devices are 32-bit elements; how exact they have to be, the bound alone decides.
No kernel may reach another device: no remote copies, remote signals or barrier semaphores. Data moves between devices by JAX's collectives and lax.ppermute only.
A program may use at most 192 MiB of HBM per device.

```python
import math
import jax
import jax.numpy as jnp
from jax import lax

VARS = 5
NZ = 8
CX = 16
CY = 128
NX = 512
NY = 2048


def draw_right_side(key, part):
    key = jax.random.fold_in(key, 11)
    amplitude = 0.326 * (1.0 * CX * CY) ** (-1.5)
    values = jnp.clip(jax.random.normal(key, (VARS, NZ, NX, NY), jnp.float32), -6.0, 6.0)
    return (values * amplitude).astype(jnp.bfloat16)


def draw_near_bands(key, part):
    key = jax.random.fold_in(key, 12)
    values = jax.random.uniform(key, (3, 2, NZ, NX, NY), jnp.float32, -0.8, -0.2)
    return values.astype(jnp.bfloat16)


def draw_margins(key, part):
    key = jax.random.fold_in(key, 13)
    first_key, second_key = jax.random.split(key)
    jitter = jax.random.uniform(first_key, (2, NZ, NX, NY), jnp.float32, -1.0, 1.0)
    widths = jnp.array([1.0 * CX * CX, 1.0 * CY * CY], jnp.float32).reshape(2, 1, 1, 1)
    planar = 0.18 * jnp.exp(jitter) / widths
    across = jnp.exp(jax.random.uniform(second_key, (1, NZ, NX, NY), jnp.float32, math.log(0.05), math.log(2.0)))
    return jnp.concatenate((planar, across), axis=0).astype(jnp.bfloat16)


def setup_inputs(seed: int = 0) -> dict:
    key_list = jax.random.split(jax.random.key(seed), 4)
    right_side = draw_right_side(jax.random.fold_in(key_list[3], 71), 0)
    near_bands = draw_near_bands(jax.random.fold_in(key_list[3], 71), 0)
    margins = draw_margins(jax.random.fold_in(key_list[3], 71), 0)
    return dict(right_side=right_side, near_bands=near_bands, margins=margins)


outer_band = -0.05


def line_solve(below_band, above_band, middle, source):
    lines = below_band.shape[1]
    columns = source.shape[1]
    zero_line = jnp.zeros((lines,), jnp.float32)
    zero_block = jnp.zeros((columns, lines), jnp.float32)

    def forward(carried, cell_row):
        near_one, near_two, near_value, far_one, far_two, far_value = carried
        sub_cell, mid_cell, sup_cell, src_cell = cell_row
        lower_term = sub_cell - outer_band * far_one
        centre = mid_cell - outer_band * far_two
        pivot_value = centre - lower_term * near_one
        ratio_one = (sup_cell - lower_term * near_two) / pivot_value
        ratio_two = outer_band / pivot_value
        reduced = (src_cell - outer_band * far_value - lower_term[None] * near_value) / pivot_value[None]
        return (ratio_one, ratio_two, reduced, near_one, near_two, near_value), (ratio_one, ratio_two, reduced)

    start = (zero_line, zero_line, zero_block, zero_line, zero_line, zero_block)
    final_state, eliminated = lax.scan(forward, start, (below_band, middle, above_band, source))

    def backward(carried, cell_row):
        next_cell, after_next = carried
        ratio_one, ratio_two, reduced = cell_row
        cell_value = reduced - ratio_one[None] * next_cell - ratio_two[None] * after_next
        return (cell_value, next_cell), cell_value

    final_state, solved = lax.scan(backward, (zero_block, zero_block), eliminated, reverse=True)
    return solved


def sweep_bands(near_bands, margins, direction):
    below_band = near_bands[direction, 0].astype(jnp.float32)
    above_band = near_bands[direction, 1].astype(jnp.float32)
    middle = jnp.abs(below_band) + jnp.abs(above_band) + 0.1 + margins[direction].astype(jnp.float32)
    return below_band, above_band, middle


def flatten_lines(coefficient, line_axis):
    return jnp.moveaxis(coefficient, line_axis, 0).reshape(coefficient.shape[line_axis], -1)


def along_lines(field, below_band, above_band, middle, line_axis):
    length_cells = field.shape[line_axis + 1]
    moved = jnp.moveaxis(field, line_axis + 1, 0)
    line_shape = moved.shape
    lines = moved.reshape(length_cells, line_shape[1], -1)
    solved = line_solve(flatten_lines(below_band, line_axis), flatten_lines(above_band, line_axis),
                        flatten_lines(middle, line_axis), lines)
    return jnp.moveaxis(solved.reshape(line_shape), 0, line_axis + 1)


def reference(right_side, near_bands, margins):
    field = right_side.astype(jnp.float32)
    field = along_lines(field, *sweep_bands(near_bands, margins, 0), 1)
    field = along_lines(field, *sweep_bands(near_bands, margins, 1), 2)
    return along_lines(field, *sweep_bands(near_bands, margins, 2), 0)
```

```python
import jax
import jax.numpy as jnp
from jax import lax
from jax.experimental import pallas as pl
from jax.experimental.pallas import tpu as pltpu
from jax.sharding import PartitionSpec as P

VARS = 5
OUTER = 0.05
F32 = jnp.float32
PARAMS = pltpu.CompilerParams(vmem_limit_bytes=48 * 1024 * 1024)

HEAD, TAIL, HEAD_IN, TAIL_IN, HEAD_OUT, TAIL_OUT = 0, 10, 20, 24, 28, 32


def solve_block(below, middle, above, sources, cells):
    count = len(sources[0])
    ratio_one, ratio_two, reduced = [], [], []
    for i in range(cells):
        sub, mid, sup = below(i), middle(i), above(i)
        zero = jnp.zeros_like(mid)
        lower = sub + OUTER * ratio_one[i - 2] if i >= 2 else sub
        centre = mid + OUTER * ratio_two[i - 2] if i >= 2 else mid
        upper = sup
        if i >= 1:
            centre = centre - lower * ratio_one[i - 1]
            upper = sup - lower * ratio_two[i - 1]
        inverse = 1.0 / centre
        row = list(sources[i])
        row.append(zero - OUTER if i == 0 else zero)
        row.append(sub if i == 0 else zero - OUTER if i == 1 else zero)
        new = []
        for c in range(count + 2):
            value = row[c]
            if i >= 2:
                value = value + OUTER * reduced[i - 2][c]
            if i >= 1:
                value = value - lower * reduced[i - 1][c]
            new.append(value * inverse)
        if i == cells - 2:
            new += [-OUTER * inverse, zero]
        elif i == cells - 1:
            new += [(sup - lower * reduced[i - 1][count + 2]) * inverse, -OUTER * inverse]
        reduced.append(new)
        ratio_one.append(upper * inverse)
        ratio_two.append(-OUTER * inverse)
    solved = [None] * cells
    solved[cells - 1] = reduced[cells - 1]
    for i in range(cells - 2, -1, -1):
        out = []
        for c in range(count + 4):
            value = reduced[i][c] if c < len(reduced[i]) else None
            term = ratio_one[i] * solved[i + 1][c]
            value = -term if value is None else value - term
            if i + 2 < cells:
                value = value - ratio_two[i] * solved[i + 2][c]
            out.append(value)
        solved[i] = out
    return solved


def relation_of(solved):
    first, second, before, last = solved[0], solved[1], solved[-2], solved[-1]
    relation = []
    for pair in ((first, second), (before, last)):
        for cell in pair:
            relation += cell[:VARS]
    for lo in (VARS, VARS + 2):
        for pair in ((first, second), (before, last)):
            for cell in pair:
                relation += cell[lo : lo + 2]
    return relation


def product(left, right):
    wide = len(right) // 2
    return [
        left[2 * r] * right[c] + left[2 * r + 1] * right[wide + c] for r in range(2) for c in range(wide)
    ]


def plus(a, b):
    return [x + y for x, y in zip(a, b)]


def minus(a, b):
    return [x - y for x, y in zip(a, b)]


def parts(relation):
    return (
        relation[HEAD:TAIL],
        relation[TAIL:HEAD_IN],
        relation[HEAD_IN:TAIL_IN],
        relation[TAIL_IN:HEAD_OUT],
        relation[HEAD_OUT:TAIL_OUT],
        relation[TAIL_OUT:],
    )


def merge(left, right):
    hv_a, tv_a, hin_a, tin_a, hout_a, tout_a = parts(left)
    hv_b, tv_b, hin_b, tin_b, hout_b, tout_b = parts(right)
    loop = product(tout_a, hin_b)
    a, b, c, d = 1.0 - loop[0], -loop[1], -loop[2], 1.0 - loop[3]
    inverse = 1.0 / (a * d - b * c)
    shift = [d * inverse, -b * inverse, -c * inverse, a * inverse]
    jv = product(shift, minus(tv_a, product(tout_a, hv_b)))
    jp = product(shift, tin_a)
    jf = product(shift, product(tout_a, hout_b))
    kv = minus(hv_b, product(hin_b, jv))
    kp = product(hin_b, jp)
    kf = plus(product(hin_b, jf), hout_b)
    merged = (
        minus(hv_a, product(hout_a, kv))
        + minus(tv_b, product(tin_b, jv))
        + plus(hin_a, product(hout_a, kp))
        + [-x for x in product(tin_b, jp)]
        + [-x for x in product(hout_a, kf)]
        + plus(product(tin_b, jf), tout_b)
    )
    return merged, jv + kv + jp + jf + kp + kf


def joint(saved, prev, following):
    jv, kv, jp, jf, kp, kf = saved[:10], saved[10:20], saved[20:24], saved[24:28], saved[28:32], saved[32:]
    tail = plus(minus(jv, product(jp, prev)), product(jf, following))
    head = minus(plus(kv, product(kp, prev)), product(kf, following))
    return tail, head


def rolled(values, shift, axis):
    return [pltpu.roll(v, shift, axis) for v in values]


def climb(relation, levels):
    kept = []
    for axis, distance, size in levels:
        relation, saved = merge(relation, rolled(relation, size - distance, axis))
        kept.append(saved)
    return relation, kept


def descend(kept, levels, prev, following):
    for saved, (axis, distance, size) in zip(reversed(kept), reversed(levels)):
        tail, head = joint(saved, prev, following)
        place = lax.broadcasted_iota(jnp.int32, (8, 128), axis)
        is_right = (place & distance) != 0
        prev = [jnp.where(is_right, pltpu.roll(t, distance, axis), p) for t, p in zip(tail, prev)]
        following = [jnp.where(is_right, pltpu.roll(f, distance, axis), h) for f, h in zip(following, head)]
    return prev, following


def swap_quarters(four):
    lane = lax.broadcasted_iota(jnp.int32, (8, 128), 1)
    low_two, low_one = (lane & 64) == 0, (lane & 32) == 0
    half = [None] * 4
    for j in (0, 1):
        a, b = four[j], four[j + 2]
        half[j] = jnp.where(low_two, a, pltpu.roll(b, 64, 1))
        half[j + 2] = jnp.where(low_two, pltpu.roll(a, 64, 1), b)
    out = [None] * 4
    for j in (0, 2):
        a, b = half[j], half[j + 1]
        out[j] = jnp.where(low_one, a, pltpu.roll(b, 32, 1))
        out[j + 1] = jnp.where(low_one, pltpu.roll(a, 96, 1), b)
    return out


ROW_LEVELS = ((1, 32, 128), (1, 64, 128), (0, 1, 8), (0, 2, 8), (0, 4, 8))
SUB_LEVELS = ((0, 1, 8), (0, 2, 8), (0, 4, 8))


def bands_of(bands_ref, margins_ref, direction):
    below = bands_ref[direction, 0].astype(F32)
    above = bands_ref[direction, 1].astype(F32)
    middle = jnp.abs(below) + jnp.abs(above) + 0.1 + margins_ref[direction].astype(F32)
    return below, middle, above


def x_local(right_ref, bands_ref, margins_ref, solved_ref, sent_ref, lines):
    below, middle, above = bands_of(bands_ref, margins_ref, 0)
    for slot, array in enumerate((below, middle, above)):
        lines[slot] = array.reshape(128, 128)
    for v in range(VARS):
        lines[3 + v] = right_ref[v].astype(F32).reshape(128, 128)

    def cell(slot):
        return lambda i: lines[slot, pl.ds(i, 8, stride=16), :]

    sources = [[cell(3 + v)(i) for v in range(VARS)] for i in range(16)]
    solved = solve_block(cell(0), cell(1), cell(2), sources, 16)
    for i in range(16):
        for c in range(VARS + 4):
            solved_ref[i, c] = solved[i][c]
    relation = relation_of(solved)
    for g in range(9):
        out = swap_quarters(relation[4 * g : 4 * g + 4])
        for quarter in range(4):
            sent_ref[pl.ds(quarter * 16 + g, 8, stride=64), :] = out[quarter]


def x_join(got_ref, sent_ref):
    relation = []
    for g in range(9):
        relation += swap_quarters([got_ref[pl.ds(quarter * 16 + g, 8, stride=64), :] for quarter in range(4)])
    _, kept = climb(relation, ROW_LEVELS)
    zero = [jnp.zeros((8, 128), F32)] * 10
    prev, following = descend(kept, ROW_LEVELS, zero, zero)
    answer = prev + following
    for g in range(5):
        out = swap_quarters(answer[4 * g : 4 * g + 4])
        for quarter in range(4):
            sent_ref[pl.ds(quarter * 8 + g, 8, stride=32), :] = out[quarter]


def with_neighbours(cell, prev, following):
    before_one, before_two, after_one, after_two = cell[VARS:]
    return [
        cell[v]
        - before_one * prev[v]
        - before_two * prev[VARS + v]
        - after_one * following[v]
        - after_two * following[VARS + v]
        for v in range(VARS)
    ]


def y_local(x_solved_ref, got_ref, bands_ref, margins_ref, solved_ref, kept_ref, sent_ref, lines, row):
    answer = []
    for g in range(5):
        answer += swap_quarters([got_ref[pl.ds(quarter * 8 + g, 8, stride=32), :] for quarter in range(4)])
    prev, following = answer[:10], answer[10:]
    for i in range(16):
        cell = [x_solved_ref[i, c] for c in range(VARS + 4)]
        for v, value in enumerate(with_neighbours(cell, prev, following)):
            lines[3 + v, pl.ds(i, 8, stride=16), :] = value
    for slot, array in enumerate(bands_of(bands_ref, margins_ref, 1)):
        lines[slot] = array.reshape(128, 128).T
    for v in range(VARS):
        lines[3 + v] = lines[3 + v].T

    def cell_of(slot):
        return lambda i: lines[slot, pl.ds(i, 8, stride=16), :]

    sources = [[cell_of(3 + v)(i) for v in range(VARS)] for i in range(16)]
    solved = solve_block(cell_of(0), cell_of(1), cell_of(2), sources, 16)
    for i in range(16):
        for c in range(VARS + 4):
            solved_ref[i, c] = solved[i][c]
    relation, kept = climb(relation_of(solved), SUB_LEVELS)
    for level in range(3):
        for c in range(36):
            kept_ref[level, c] = kept[level][c]
    for c in range(36):
        row[c : c + 1, :] = relation[c][0:1, :]
    whole = row[...]
    for j in range(16):
        sent_ref[pl.ds(j * 40, 40), :] = whole


def y_join(got_ref, y_solved_ref, kept_ref, bands_ref, margins_ref, out_ref, lines, row):
    mine = lax.axis_index("col")
    even = [got_ref[pl.ds(c, 8, stride=80), :] for c in range(36)]
    odd = [got_ref[pl.ds(40 + c, 8, stride=80), :] for c in range(36)]
    relation, pair = merge(even, odd)
    _, kept = climb(relation, SUB_LEVELS)
    zero = [jnp.zeros((8, 128), F32)] * 10
    prev, following = descend(kept, SUB_LEVELS, zero, zero)
    tail, head = joint(pair, prev, following)
    is_odd = jnp.full((8, 128), mine % 2, jnp.int32) != 0
    prev = [jnp.where(is_odd, t, p) for t, p in zip(tail, prev)]
    following = [jnp.where(is_odd, f, h) for f, h in zip(following, head)]
    for c, value in enumerate(prev + following):
        row[c] = value
    place = mine // 2
    own = [jnp.broadcast_to(row[c, pl.ds(place, 1), :], (8, 128)) for c in range(20)]
    kept = [[kept_ref[level, c] for c in range(36)] for level in range(3)]
    prev, following = descend(kept, SUB_LEVELS, own[:10], own[10:])
    for i in range(16):
        cell = [y_solved_ref[i, c] for c in range(VARS + 4)]
        for v, value in enumerate(with_neighbours(cell, prev, following)):
            lines[v, pl.ds(i, 8, stride=16), :] = value
    below, middle, above = bands_of(bands_ref, margins_ref, 2)
    ratio_one, ratio_two, reduced = [], [], []
    fields = [lines[v].T.reshape(8, 16, 128) for v in range(VARS)]
    for i in range(8):
        lower = below[i] + OUTER * ratio_one[i - 2] if i >= 2 else below[i]
        centre = middle[i] + OUTER * ratio_two[i - 2] if i >= 2 else middle[i]
        upper = above[i]
        if i >= 1:
            centre = centre - lower * ratio_one[i - 1]
            upper = upper - lower * ratio_two[i - 1]
        inverse = 1.0 / centre
        new = []
        for v in range(VARS):
            value = fields[v][i]
            if i >= 2:
                value = value + OUTER * reduced[i - 2][v]
            if i >= 1:
                value = value - lower * reduced[i - 1][v]
            new.append(value * inverse)
        reduced.append(new)
        ratio_one.append(upper * inverse)
        ratio_two.append(-OUTER * inverse)
    later = [None, None]
    for i in range(7, -1, -1):
        now = []
        for v in range(VARS):
            value = reduced[i][v]
            if later[0] is not None:
                value = value - ratio_one[i] * later[0][v]
            if later[1] is not None:
                value = value - ratio_two[i] * later[1][v]
            now.append(value)
            out_ref[v, i] = value
        later = [now, later[0]]


def call(kernel, outs, scratch):
    return pl.pallas_call(
        kernel,
        out_shape=[jax.ShapeDtypeStruct(shape, F32) for shape in outs],
        scratch_shapes=[pltpu.VMEM(shape, F32) for shape in scratch],
        compiler_params=PARAMS,
    )


def exchange(array, axis, count):
    array = array.reshape(count, -1, 128)
    return lax.all_to_all(array, axis, 0, 0, tiled=True).reshape(-1, 128)


def body(right_side, near_bands, margins):
    x_solved, sent = call(x_local, [(16, 9, 8, 128), (512, 128)], [(8, 128, 128)])(
        right_side, near_bands, margins
    )
    (answer,) = call(x_join, [(256, 128)], [])(exchange(sent, "row", 32))
    y_solved, kept, sent = call(
        y_local, [(16, 9, 8, 128), (3, 36, 8, 128), (640, 128)], [(8, 128, 128), (40, 128)]
    )(x_solved, exchange(answer, "row", 32), near_bands, margins)
    (update,) = call(y_join, [(VARS, 8, 16, 128)], [(VARS, 128, 128), (20, 8, 128)])(
        exchange(sent, "col", 16), y_solved, kept, near_bands, margins
    )
    return update


def solution(mesh):
    placed = (
        P(None, None, "row", "col"),
        P(None, None, None, "row", "col"),
        P(None, None, "row", "col"),
    )
    return jax.shard_map(
        body, mesh=mesh, in_specs=placed, out_specs=P(None, None, "row", "col"), check_vma=False
    )
```

```python
import jax
import jax.numpy as jnp
from jax import lax
from jax.experimental import pallas as pl
from jax.experimental.pallas import tpu as pltpu
from jax.sharding import PartitionSpec as P

VARS = 5
OUTER = 0.05
F32 = jnp.float32
PARAMS = pltpu.CompilerParams(vmem_limit_bytes=48 * 1024 * 1024)

HEAD, TAIL, HEAD_IN, TAIL_IN, HEAD_OUT, TAIL_OUT = 0, 10, 20, 24, 28, 32


def solve_block(below, middle, above, sources, cells):
    count = len(sources[0])
    ratio_one, ratio_two, reduced = [], [], []
    for i in range(cells):
        sub, mid, sup = below(i), middle(i), above(i)
        zero = jnp.zeros_like(mid)
        lower = sub + OUTER * ratio_one[i - 2] if i >= 2 else sub
        centre = mid + OUTER * ratio_two[i - 2] if i >= 2 else mid
        upper = sup
        if i >= 1:
            centre = centre - lower * ratio_one[i - 1]
            upper = sup - lower * ratio_two[i - 1]
        inverse = 1.0 / centre
        row = list(sources[i])
        row.append(zero - OUTER if i == 0 else zero)
        row.append(sub if i == 0 else zero - OUTER if i == 1 else zero)
        new = []
        for c in range(count + 2):
            value = row[c]
            if i >= 2:
                value = value + OUTER * reduced[i - 2][c]
            if i >= 1:
                value = value - lower * reduced[i - 1][c]
            new.append(value * inverse)
        if i == cells - 2:
            new += [-OUTER * inverse, zero]
        elif i == cells - 1:
            new += [(sup - lower * reduced[i - 1][count + 2]) * inverse, -OUTER * inverse]
        reduced.append(new)
        ratio_one.append(upper * inverse)
        ratio_two.append(-OUTER * inverse)
    solved = [None] * cells
    solved[cells - 1] = reduced[cells - 1]
    for i in range(cells - 2, -1, -1):
        out = []
        for c in range(count + 4):
            value = reduced[i][c] if c < len(reduced[i]) else None
            term = ratio_one[i] * solved[i + 1][c]
            value = -term if value is None else value - term
            if i + 2 < cells:
                value = value - ratio_two[i] * solved[i + 2][c]
            out.append(value)
        solved[i] = out
    return solved


def relation_of(solved):
    first, second, before, last = solved[0], solved[1], solved[-2], solved[-1]
    relation = []
    for pair in ((first, second), (before, last)):
        for cell in pair:
            relation += cell[:VARS]
    for lo in (VARS, VARS + 2):
        for pair in ((first, second), (before, last)):
            for cell in pair:
                relation += cell[lo : lo + 2]
    return relation


def product(left, right):
    wide = len(right) // 2
    return [
        left[2 * r] * right[c] + left[2 * r + 1] * right[wide + c] for r in range(2) for c in range(wide)
    ]


def plus(a, b):
    return [x + y for x, y in zip(a, b)]


def minus(a, b):
    return [x - y for x, y in zip(a, b)]


def parts(relation):
    return (
        relation[HEAD:TAIL],
        relation[TAIL:HEAD_IN],
        relation[HEAD_IN:TAIL_IN],
        relation[TAIL_IN:HEAD_OUT],
        relation[HEAD_OUT:TAIL_OUT],
        relation[TAIL_OUT:],
    )


def merge(left, right):
    hv_a, tv_a, hin_a, tin_a, hout_a, tout_a = parts(left)
    hv_b, tv_b, hin_b, tin_b, hout_b, tout_b = parts(right)
    loop = product(tout_a, hin_b)
    a, b, c, d = 1.0 - loop[0], -loop[1], -loop[2], 1.0 - loop[3]
    inverse = 1.0 / (a * d - b * c)
    shift = [d * inverse, -b * inverse, -c * inverse, a * inverse]
    jv = product(shift, minus(tv_a, product(tout_a, hv_b)))
    jp = product(shift, tin_a)
    jf = product(shift, product(tout_a, hout_b))
    kv = minus(hv_b, product(hin_b, jv))
    kp = product(hin_b, jp)
    kf = plus(product(hin_b, jf), hout_b)
    merged = (
        minus(hv_a, product(hout_a, kv))
        + minus(tv_b, product(tin_b, jv))
        + plus(hin_a, product(hout_a, kp))
        + [-x for x in product(tin_b, jp)]
        + [-x for x in product(hout_a, kf)]
        + plus(product(tin_b, jf), tout_b)
    )
    return merged, jv + kv + jp + jf + kp + kf


def joint(saved, prev, following):
    jv, kv, jp, jf, kp, kf = saved[:10], saved[10:20], saved[20:24], saved[24:28], saved[28:32], saved[32:]
    tail = plus(minus(jv, product(jp, prev)), product(jf, following))
    head = minus(plus(kv, product(kp, prev)), product(kf, following))
    return tail, head


def rolled(values, shift, axis):
    return [pltpu.roll(v, shift, axis) for v in values]


def climb(relation, levels):
    kept = []
    for axis, distance, size in levels:
        relation, saved = merge(relation, rolled(relation, size - distance, axis))
        kept.append(saved)
    return relation, kept


def descend(kept, levels, prev, following):
    for saved, (axis, distance, size) in zip(reversed(kept), reversed(levels)):
        tail, head = joint(saved, prev, following)
        place = lax.broadcasted_iota(jnp.int32, (8, 128), axis)
        is_right = (place & distance) != 0
        prev = [jnp.where(is_right, pltpu.roll(t, distance, axis), p) for t, p in zip(tail, prev)]
        following = [jnp.where(is_right, pltpu.roll(f, distance, axis), h) for f, h in zip(following, head)]
    return prev, following


RING_ORDER, ACROSS_ORDER, DEEP_ORDER = (4, 3, 5, 2, 6, 1, 7, 0), (2, 1, 3, 0), (6, 7, 5, 4, 3, 2, 1, 0)
RING = [[8 * x + y for y in RING_ORDER] for x in range(4)]
ACROSS = [[8 * x + y for x in ACROSS_ORDER] for y in range(8)]
DEEP = [[2 * z + core for z in DEEP_ORDER] for core in range(2)]
CORES = [[2 * z, 2 * z + 1] for z in range(8)]

FOUR_LEVELS = ((0, 1, 8), (0, 2, 8))
SUB_LEVELS = ((0, 1, 8), (0, 2, 8), (0, 4, 8))


def bands_of(bands_ref, margins_ref, direction):
    below = bands_ref[direction, 0].astype(F32)
    above = bands_ref[direction, 1].astype(F32)
    middle = jnp.abs(below) + jnp.abs(above) + 0.1 + margins_ref[direction].astype(F32)
    return below, middle, above


def x_local(right_hbm, bands_hbm, margins_hbm, solved_ref, sent_ref, lines, right, bands, margins, arrived):
    copies = [
        pltpu.make_async_copy(bands_hbm.at[0], bands, arrived.at[0]),
        pltpu.make_async_copy(margins_hbm.at[0], margins, arrived.at[1]),
        pltpu.make_async_copy(right_hbm, right, arrived.at[2]),
    ]
    for copy in copies:
        copy.start()
    copies[0].wait()
    copies[1].wait()
    below, above = bands[0].astype(F32), bands[1].astype(F32)
    middle = jnp.abs(below) + jnp.abs(above) + 0.1 + margins[...].astype(F32)
    for slot, array in enumerate((below, middle, above)):
        lines[slot] = array.reshape(128, 128)
    copies[2].wait()
    for v in range(VARS):
        lines[3 + v] = right[v].astype(F32).reshape(128, 128)

    def cell(slot):
        return lambda i: lines[slot, pl.ds(i, 8, stride=16), :]

    sources = [[cell(3 + v)(i) for v in range(VARS)] for i in range(16)]
    solved = solve_block(cell(0), cell(1), cell(2), sources, 16)
    for i in range(16):
        for c in range(VARS + 4):
            solved_ref[i, c] = solved[i][c]
    relation = relation_of(solved)
    for c in range(36):
        sent_ref[pl.ds(c, 8, stride=40), :] = relation[c]


def send_to_all(relation, sent_ref, row, count):
    row[...] = jnp.zeros_like(row)
    for c in range(36):
        row[c : c + 1, :] = relation[c][0:1, :]
    whole = row[...]
    for j in range(count):
        sent_ref[pl.ds(j * 40, 40), :] = whole


def own_part(values, place, row):
    for c, value in enumerate(values):
        row[c] = value
    return [jnp.broadcast_to(row[c, pl.ds(place, 1), :], (8, 128)) for c in range(len(values))]


def in_order(got_ref, ordered, order):
    for position, member in enumerate(order):
        ordered[member * 40 : member * 40 + 40, :] = got_ref[position * 40 : position * 40 + 40, :]
    return [ordered[pl.ds(c, 8, stride=40), :] for c in range(36)]


def x_ring(got_ref, kept_ref, sent_ref, row, ordered):
    relation, kept = climb(in_order(got_ref, ordered, RING_ORDER), SUB_LEVELS)
    for level in range(3):
        for c in range(36):
            kept_ref[level, c] = kept[level][c]
    send_to_all(relation, sent_ref, row, 4)


def x_join(got_ref, kept_ref, sent_ref, twice, row, ordered):
    for half in range(2):
        for position, member in enumerate(ACROSS_ORDER):
            start = half * 160 + member * 40
            twice[start : start + 40, :] = got_ref[position * 40 : position * 40 + 40, :]
    _, kept = climb([twice[pl.ds(c, 8, stride=40), :] for c in range(36)], FOUR_LEVELS)
    zero = [jnp.zeros((8, 128), F32)] * 10
    prev, following = descend(kept, FOUR_LEVELS, zero, zero)
    own = own_part(prev + following, lax.axis_index("row") // 8, row)
    kept = [[kept_ref[level, c] for c in range(36)] for level in range(3)]
    prev, following = descend(kept, SUB_LEVELS, own[:10], own[10:])
    for c, value in enumerate(prev + following):
        ordered[pl.ds(c, 8, stride=24), :] = value
    for position, member in enumerate(RING_ORDER):
        sent_ref[position * 24 : position * 24 + 24, :] = ordered[member * 24 : member * 24 + 24, :]


def with_neighbours(cell, prev, following):
    before_one, before_two, after_one, after_two = cell[VARS:]
    return [
        cell[v]
        - before_one * prev[v]
        - before_two * prev[VARS + v]
        - after_one * following[v]
        - after_two * following[VARS + v]
        for v in range(VARS)
    ]


def y_local(x_solved_ref, got_ref, bands_ref, margins_ref, solved_ref, kept_ref, sent_ref, lines, row):
    answer = [got_ref[pl.ds(c, 8, stride=24), :] for c in range(20)]
    prev, following = answer[:10], answer[10:]
    for i in range(16):
        cell = [x_solved_ref[i, c] for c in range(VARS + 4)]
        for v, value in enumerate(with_neighbours(cell, prev, following)):
            lines[3 + v, pl.ds(i, 8, stride=16), :] = value
    for slot, array in enumerate(bands_of(bands_ref, margins_ref, 1)):
        lines[slot] = array.reshape(128, 128).T
    for v in range(VARS):
        lines[3 + v] = lines[3 + v].T

    def cell_of(slot):
        return lambda i: lines[slot, pl.ds(i, 8, stride=16), :]

    sources = [[cell_of(3 + v)(i) for v in range(VARS)] for i in range(16)]
    solved = solve_block(cell_of(0), cell_of(1), cell_of(2), sources, 16)
    for i in range(16):
        for c in range(VARS + 4):
            solved_ref[i, c] = solved[i][c]
    relation, kept = climb(relation_of(solved), SUB_LEVELS)
    for level in range(3):
        for c in range(36):
            kept_ref[level, c] = kept[level][c]
    send_to_all(relation, sent_ref, row, 1)


def y_pair(got_ref, pair_ref, sent_ref, row):
    left, right = ([got_ref[40 * s + c : 40 * s + c + 1, :] for c in range(36)] for s in range(2))
    relation, pair = merge(left, right)
    for c in range(36):
        pair_ref[c : c + 1, :] = pair[c]
    send_to_all(relation, sent_ref, row, 8)


def y_join(got_ref, pair_ref, y_solved_ref, kept_ref, bands_ref, margins_ref, out_ref, lines, row, ordered):
    mine = lax.axis_index("col")
    _, kept = climb(in_order(got_ref, ordered, DEEP_ORDER), SUB_LEVELS)
    zero = [jnp.zeros((8, 128), F32)] * 10
    prev, following = descend(kept, SUB_LEVELS, zero, zero)
    own = own_part(prev + following, mine // 2, row)
    prev, following = own[:10], own[10:]
    tail, head = joint([pair_ref[c : c + 1, :] for c in range(36)], prev, following)
    is_right = jnp.full((8, 128), mine % 2, jnp.int32) != 0
    own = [jnp.where(is_right, t, p) for t, p in zip(tail, prev)]
    own += [jnp.where(is_right, f, h) for f, h in zip(following, head)]
    kept = [[kept_ref[level, c] for c in range(36)] for level in range(3)]
    prev, following = descend(kept, SUB_LEVELS, own[:10], own[10:])
    for i in range(16):
        cell = [y_solved_ref[i, c] for c in range(VARS + 4)]
        for v, value in enumerate(with_neighbours(cell, prev, following)):
            lines[v, pl.ds(i, 8, stride=16), :] = value
    below, middle, above = bands_of(bands_ref, margins_ref, 2)
    ratio_one, ratio_two, reduced = [], [], []
    fields = [lines[v].T.reshape(8, 16, 128) for v in range(VARS)]
    for i in range(8):
        lower = below[i] + OUTER * ratio_one[i - 2] if i >= 2 else below[i]
        centre = middle[i] + OUTER * ratio_two[i - 2] if i >= 2 else middle[i]
        upper = above[i]
        if i >= 1:
            centre = centre - lower * ratio_one[i - 1]
            upper = upper - lower * ratio_two[i - 1]
        inverse = 1.0 / centre
        new = []
        for v in range(VARS):
            value = fields[v][i]
            if i >= 2:
                value = value + OUTER * reduced[i - 2][v]
            if i >= 1:
                value = value - lower * reduced[i - 1][v]
            new.append(value * inverse)
        reduced.append(new)
        ratio_one.append(upper * inverse)
        ratio_two.append(-OUTER * inverse)
    later = [None, None]
    for i in range(7, -1, -1):
        now = []
        for v in range(VARS):
            value = reduced[i][v]
            if later[0] is not None:
                value = value - ratio_one[i] * later[0][v]
            if later[1] is not None:
                value = value - ratio_two[i] * later[1][v]
            now.append(value)
            out_ref[v, i] = value
        later = [now, later[0]]


def call(kernel, outs, scratch):
    return pl.pallas_call(
        kernel,
        out_shape=[jax.ShapeDtypeStruct(shape, F32) for shape in outs],
        scratch_shapes=[pltpu.VMEM(shape, F32) for shape in scratch],
        compiler_params=PARAMS,
    )


def exchange(array, axis, count, members=None):
    array = array.reshape(count, -1, 128)
    return lax.all_to_all(array, axis, 0, 0, tiled=True, axis_index_groups=members).reshape(-1, 128)


def body(right_side, near_bands, margins):
    x_solved, sent = pl.pallas_call(
        x_local,
        in_specs=[pl.BlockSpec(memory_space=pltpu.HBM)] * 3,
        out_shape=[jax.ShapeDtypeStruct((16, 9, 8, 128), F32), jax.ShapeDtypeStruct((320, 128), F32)],
        scratch_shapes=[
            pltpu.VMEM((8, 128, 128), F32),
            pltpu.VMEM((VARS, 8, 16, 128), jnp.bfloat16),
            pltpu.VMEM((2, 8, 16, 128), jnp.bfloat16),
            pltpu.VMEM((8, 16, 128), jnp.bfloat16),
            pltpu.SemaphoreType.DMA((3,)),
        ],
        compiler_params=PARAMS,
    )(*[pltpu.with_memory_space_constraint(a, pltpu.HBM) for a in (right_side, near_bands, margins)])
    kept, sent = call(x_ring, [(3, 36, 8, 128), (160, 128)], [(40, 128), (320, 128)])(exchange(sent, "row", 8, RING))
    (answer,) = call(x_join, [(192, 128)], [(320, 128), (20, 8, 128), (192, 128)])(exchange(sent, "row", 4, ACROSS), kept)
    y_solved, kept, sent = call(
        y_local, [(16, 9, 8, 128), (3, 36, 8, 128), (40, 128)], [(8, 128, 128), (40, 128)]
    )(x_solved, exchange(answer, "row", 8, RING), near_bands, margins)
    both = lax.all_gather(sent, "col", axis_index_groups=CORES, tiled=True)
    pair, sent = call(y_pair, [(36, 128), (320, 128)], [(40, 128)])(both)
    (update,) = call(y_join, [(VARS, 8, 16, 128)], [(VARS, 128, 128), (20, 8, 128), (320, 128)])(
        exchange(sent, "col", 8, DEEP), pair, y_solved, kept, near_bands, margins
    )
    return update


def solution(mesh):
    placed = (
        P(None, None, "row", "col"),
        P(None, None, None, "row", "col"),
        P(None, None, "row", "col"),
    )
    return jax.shard_map(
        body, mesh=mesh, in_specs=placed, out_specs=P(None, None, "row", "col"), check_vma=False
    )
```

```python
import jax
import jax.numpy as jnp
from jax import lax
from jax.experimental import pallas as pl
from jax.experimental.pallas import tpu as pltpu
from jax.sharding import PartitionSpec as P

VARS = 5
OUTER = 0.05
F32 = jnp.float32
PARAMS = pltpu.CompilerParams(vmem_limit_bytes=48 * 1024 * 1024)

HEAD, TAIL, HEAD_IN, TAIL_IN, HEAD_OUT, TAIL_OUT = 0, 10, 20, 24, 28, 32


def solve_block(below, middle, above, sources, cells):
    count = len(sources[0])
    ratio_one, ratio_two, reduced = [], [], []
    for i in range(cells):
        sub, mid, sup = below(i), middle(i), above(i)
        zero = jnp.zeros_like(mid)
        lower = sub + OUTER * ratio_one[i - 2] if i >= 2 else sub
        centre = mid + OUTER * ratio_two[i - 2] if i >= 2 else mid
        upper = sup
        if i >= 1:
            centre = centre - lower * ratio_one[i - 1]
            upper = sup - lower * ratio_two[i - 1]
        inverse = 1.0 / centre
        row = list(sources[i])
        row.append(zero - OUTER if i == 0 else zero)
        row.append(sub if i == 0 else zero - OUTER if i == 1 else zero)
        new = []
        for c in range(count + 2):
            value = row[c]
            if i >= 2:
                value = value + OUTER * reduced[i - 2][c]
            if i >= 1:
                value = value - lower * reduced[i - 1][c]
            new.append(value * inverse)
        if i == cells - 2:
            new += [-OUTER * inverse, zero]
        elif i == cells - 1:
            new += [(sup - lower * reduced[i - 1][count + 2]) * inverse, -OUTER * inverse]
        reduced.append(new)
        ratio_one.append(upper * inverse)
        ratio_two.append(-OUTER * inverse)
    solved = [None] * cells
    solved[cells - 1] = reduced[cells - 1]
    for i in range(cells - 2, -1, -1):
        out = []
        for c in range(count + 4):
            value = reduced[i][c] if c < len(reduced[i]) else None
            term = ratio_one[i] * solved[i + 1][c]
            value = -term if value is None else value - term
            if i + 2 < cells:
                value = value - ratio_two[i] * solved[i + 2][c]
            out.append(value)
        solved[i] = out
    return solved


def relation_of(solved):
    first, second, before, last = solved[0], solved[1], solved[-2], solved[-1]
    relation = []
    for pair in ((first, second), (before, last)):
        for cell in pair:
            relation += cell[:VARS]
    for lo in (VARS, VARS + 2):
        for pair in ((first, second), (before, last)):
            for cell in pair:
                relation += cell[lo : lo + 2]
    return relation


def product(left, right):
    wide = len(right) // 2
    return [
        left[2 * r] * right[c] + left[2 * r + 1] * right[wide + c] for r in range(2) for c in range(wide)
    ]


def plus(a, b):
    return [x + y for x, y in zip(a, b)]


def minus(a, b):
    return [x - y for x, y in zip(a, b)]


def parts(relation):
    return (
        relation[HEAD:TAIL],
        relation[TAIL:HEAD_IN],
        relation[HEAD_IN:TAIL_IN],
        relation[TAIL_IN:HEAD_OUT],
        relation[HEAD_OUT:TAIL_OUT],
        relation[TAIL_OUT:],
    )


def merge(left, right):
    hv_a, tv_a, hin_a, tin_a, hout_a, tout_a = parts(left)
    hv_b, tv_b, hin_b, tin_b, hout_b, tout_b = parts(right)
    loop = product(tout_a, hin_b)
    a, b, c, d = 1.0 - loop[0], -loop[1], -loop[2], 1.0 - loop[3]
    inverse = 1.0 / (a * d - b * c)
    shift = [d * inverse, -b * inverse, -c * inverse, a * inverse]
    jv = product(shift, minus(tv_a, product(tout_a, hv_b)))
    jp = product(shift, tin_a)
    jf = product(shift, product(tout_a, hout_b))
    kv = minus(hv_b, product(hin_b, jv))
    kp = product(hin_b, jp)
    kf = plus(product(hin_b, jf), hout_b)
    merged = (
        minus(hv_a, product(hout_a, kv))
        + minus(tv_b, product(tin_b, jv))
        + plus(hin_a, product(hout_a, kp))
        + [-x for x in product(tin_b, jp)]
        + [-x for x in product(hout_a, kf)]
        + plus(product(tin_b, jf), tout_b)
    )
    return merged, jv + kv + jp + jf + kp + kf


def joint(saved, prev, following):
    jv, kv, jp, jf, kp, kf = saved[:10], saved[10:20], saved[20:24], saved[24:28], saved[28:32], saved[32:]
    tail = plus(minus(jv, product(jp, prev)), product(jf, following))
    head = minus(plus(kv, product(kp, prev)), product(kf, following))
    return tail, head


def rolled(values, shift, axis):
    return [pltpu.roll(v, shift, axis) for v in values]


def climb(relation, levels):
    kept = []
    for axis, distance, size, mirrored in levels:
        other = rolled(relation, size - distance, axis)
        relation, saved = merge(other, relation) if mirrored else merge(relation, other)
        kept.append(saved)
    return relation, kept


def descend(kept, levels, prev, following):
    for saved, (axis, distance, size, mirrored) in zip(reversed(kept), reversed(levels)):
        tail, head = joint(saved, prev, following)
        place = lax.broadcasted_iota(jnp.int32, (8, 128), axis)
        far = (place & distance) != 0
        if mirrored:
            prev = [jnp.where(far, pltpu.roll(p, distance, axis), t) for t, p in zip(tail, prev)]
            following = [jnp.where(far, pltpu.roll(h, distance, axis), f) for f, h in zip(following, head)]
        else:
            prev = [jnp.where(far, pltpu.roll(t, distance, axis), p) for t, p in zip(tail, prev)]
            following = [jnp.where(far, pltpu.roll(f, distance, axis), h) for f, h in zip(following, head)]
    return prev, following


def swap_quarters(four):
    lane = lax.broadcasted_iota(jnp.int32, (8, 128), 1)
    low_two, low_one = (lane & 64) == 0, (lane & 32) == 0
    half = [None] * 4
    for j in (0, 1):
        a, b = four[j], four[j + 2]
        half[j] = jnp.where(low_two, a, pltpu.roll(b, 64, 1))
        half[j + 2] = jnp.where(low_two, pltpu.roll(a, 64, 1), b)
    out = [None] * 4
    for j in (0, 2):
        a, b = half[j], half[j + 1]
        out[j] = jnp.where(low_one, a, pltpu.roll(b, 32, 1))
        out[j + 1] = jnp.where(low_one, pltpu.roll(a, 96, 1), b)
    return out


ROW_MASK, DEEP_MASK = 20, 6
ROWS = [[k ^ ROW_MASK for k in range(32)]]
DEEP = [[2 * (k ^ DEEP_MASK) + core for k in range(8)] for core in range(2)]
CORES = [[2 * z, 2 * z + 1] for z in range(8)]

SUB_LEVELS = tuple((0, 1 << bit, 8, False) for bit in range(3))
DEEP_LEVELS = tuple((0, 1 << bit, 8, bool(DEEP_MASK >> bit & 1)) for bit in range(3))
ROW_LEVELS = tuple((1, 32 << bit, 128, bool(ROW_MASK >> bit & 1)) for bit in range(2))
ROW_LEVELS += tuple((0, 1 << bit, 8, bool(ROW_MASK >> bit + 2 & 1)) for bit in range(3))


def bands_of(bands_ref, margins_ref, direction):
    below = bands_ref[direction, 0].astype(F32)
    above = bands_ref[direction, 1].astype(F32)
    middle = jnp.abs(below) + jnp.abs(above) + 0.1 + margins_ref[direction].astype(F32)
    return below, middle, above


def x_local(right_hbm, bands_hbm, margins_hbm, solved_ref, sent_ref, lines, right, bands, margins, arrived):
    copies = [
        pltpu.make_async_copy(bands_hbm.at[0], bands, arrived.at[0]),
        pltpu.make_async_copy(margins_hbm.at[0], margins, arrived.at[1]),
        pltpu.make_async_copy(right_hbm, right, arrived.at[2]),
    ]
    for copy in copies:
        copy.start()
    copies[0].wait()
    copies[1].wait()
    below, above = bands[0].astype(F32), bands[1].astype(F32)
    middle = jnp.abs(below) + jnp.abs(above) + 0.1 + margins[...].astype(F32)
    for slot, array in enumerate((below, middle, above)):
        lines[slot] = array.reshape(128, 128)
    copies[2].wait()
    for v in range(VARS):
        lines[3 + v] = right[v].astype(F32).reshape(128, 128)

    def cell(slot):
        return lambda i: lines[slot, pl.ds(i, 8, stride=16), :]

    sources = [[cell(3 + v)(i) for v in range(VARS)] for i in range(16)]
    solved = solve_block(cell(0), cell(1), cell(2), sources, 16)
    for i in range(16):
        for c in range(VARS + 4):
            solved_ref[i, c] = solved[i][c]
    relation = relation_of(solved)
    for g in range(9):
        out = swap_quarters(relation[4 * g : 4 * g + 4])
        for quarter in range(4):
            sent_ref[pl.ds(quarter * 9 + g, 8, stride=36), :] = out[quarter]


def send_to_all(relation, sent_ref, row, count):
    for c in range(36):
        row[c : c + 1, :] = relation[c][0:1, :]
    whole = row[...]
    for j in range(count):
        sent_ref[j * 36 : j * 36 + 36, :] = whole


def own_part(values, place, row):
    for c, value in enumerate(values):
        row[c] = value
    return [jnp.broadcast_to(row[c, pl.ds(place, 1), :], (8, 128)) for c in range(len(values))]


def x_join(got_ref, sent_ref):
    relation = []
    for g in range(9):
        relation += swap_quarters([got_ref[pl.ds(quarter * 9 + g, 8, stride=36), :] for quarter in range(4)])
    _, kept = climb(relation, ROW_LEVELS)
    zero = [jnp.zeros((8, 128), F32)] * 10
    prev, following = descend(kept, ROW_LEVELS, zero, zero)
    answer = prev + following
    for g in range(5):
        out = swap_quarters(answer[4 * g : 4 * g + 4])
        for quarter in range(4):
            sent_ref[pl.ds(quarter * 5 + g, 8, stride=20), :] = out[quarter]


def with_neighbours(cell, prev, following):
    before_one, before_two, after_one, after_two = cell[VARS:]
    return [
        cell[v]
        - before_one * prev[v]
        - before_two * prev[VARS + v]
        - after_one * following[v]
        - after_two * following[VARS + v]
        for v in range(VARS)
    ]


def y_local(x_solved_ref, got_ref, bands_ref, margins_ref, solved_ref, kept_ref, sent_ref, lines, row):
    answer = []
    for g in range(5):
        answer += swap_quarters([got_ref[pl.ds(quarter * 5 + g, 8, stride=20), :] for quarter in range(4)])
    prev, following = answer[:10], answer[10:]
    for i in range(16):
        cell = [x_solved_ref[i, c] for c in range(VARS + 4)]
        for v, value in enumerate(with_neighbours(cell, prev, following)):
            lines[3 + v, pl.ds(i, 8, stride=16), :] = value
    for slot, array in enumerate(bands_of(bands_ref, margins_ref, 1)):
        lines[slot] = array.reshape(128, 128).T
    for v in range(VARS):
        lines[3 + v] = lines[3 + v].T

    def cell_of(slot):
        return lambda i: lines[slot, pl.ds(i, 8, stride=16), :]

    sources = [[cell_of(3 + v)(i) for v in range(VARS)] for i in range(16)]
    solved = solve_block(cell_of(0), cell_of(1), cell_of(2), sources, 16)
    for i in range(16):
        for c in range(VARS + 4):
            solved_ref[i, c] = solved[i][c]
    relation, kept = climb(relation_of(solved), SUB_LEVELS)
    for level in range(3):
        for c in range(36):
            kept_ref[level, c] = kept[level][c]
    send_to_all(relation, sent_ref, row, 1)


def y_pair(got_ref, pair_ref, sent_ref, row):
    left, right = ([got_ref[36 * s + c : 36 * s + c + 1, :] for c in range(36)] for s in range(2))
    relation, pair = merge(left, right)
    for c in range(36):
        pair_ref[c : c + 1, :] = pair[c]
    send_to_all(relation, sent_ref, row, 8)


def y_join(got_ref, pair_ref, y_solved_ref, kept_ref, bands_ref, margins_ref, out_ref, lines, row):
    mine = lax.axis_index("col")
    _, kept = climb([got_ref[pl.ds(c, 8, stride=36), :] for c in range(36)], DEEP_LEVELS)
    zero = [jnp.zeros((8, 128), F32)] * 10
    prev, following = descend(kept, DEEP_LEVELS, zero, zero)
    own = own_part(prev + following, (mine // 2) ^ DEEP_MASK, row)
    prev, following = own[:10], own[10:]
    tail, head = joint([pair_ref[c : c + 1, :] for c in range(36)], prev, following)
    is_right = jnp.full((8, 128), mine % 2, jnp.int32) != 0
    own = [jnp.where(is_right, t, p) for t, p in zip(tail, prev)]
    own += [jnp.where(is_right, f, h) for f, h in zip(following, head)]
    kept = [[kept_ref[level, c] for c in range(36)] for level in range(3)]
    prev, following = descend(kept, SUB_LEVELS, own[:10], own[10:])
    for i in range(16):
        cell = [y_solved_ref[i, c] for c in range(VARS + 4)]
        for v, value in enumerate(with_neighbours(cell, prev, following)):
            lines[v, pl.ds(i, 8, stride=16), :] = value
    below, middle, above = bands_of(bands_ref, margins_ref, 2)
    ratio_one, ratio_two, reduced = [], [], []
    fields = [lines[v].T.reshape(8, 16, 128) for v in range(VARS)]
    for i in range(8):
        lower = below[i] + OUTER * ratio_one[i - 2] if i >= 2 else below[i]
        centre = middle[i] + OUTER * ratio_two[i - 2] if i >= 2 else middle[i]
        upper = above[i]
        if i >= 1:
            centre = centre - lower * ratio_one[i - 1]
            upper = upper - lower * ratio_two[i - 1]
        inverse = 1.0 / centre
        new = []
        for v in range(VARS):
            value = fields[v][i]
            if i >= 2:
                value = value + OUTER * reduced[i - 2][v]
            if i >= 1:
                value = value - lower * reduced[i - 1][v]
            new.append(value * inverse)
        reduced.append(new)
        ratio_one.append(upper * inverse)
        ratio_two.append(-OUTER * inverse)
    later = [None, None]
    for i in range(7, -1, -1):
        now = []
        for v in range(VARS):
            value = reduced[i][v]
            if later[0] is not None:
                value = value - ratio_one[i] * later[0][v]
            if later[1] is not None:
                value = value - ratio_two[i] * later[1][v]
            now.append(value)
            out_ref[v, i] = value
        later = [now, later[0]]


def call(kernel, outs, scratch):
    return pl.pallas_call(
        kernel,
        out_shape=[jax.ShapeDtypeStruct(shape, F32) for shape in outs],
        scratch_shapes=[pltpu.VMEM(shape, F32) for shape in scratch],
        compiler_params=PARAMS,
    )


def exchange(array, axis, members, rows):
    array = array.reshape(len(members[0]), -1, rows, 128)
    return lax.all_to_all(array, axis, 0, 0, tiled=True, axis_index_groups=members).reshape(-1, 128)


def body(right_side, near_bands, margins):
    x_solved, sent = pl.pallas_call(
        x_local,
        in_specs=[pl.BlockSpec(memory_space=pltpu.HBM)] * 3,
        out_shape=[jax.ShapeDtypeStruct((16, 9, 8, 128), F32), jax.ShapeDtypeStruct((288, 128), F32)],
        scratch_shapes=[
            pltpu.VMEM((8, 128, 128), F32),
            pltpu.VMEM((VARS, 8, 16, 128), jnp.bfloat16),
            pltpu.VMEM((2, 8, 16, 128), jnp.bfloat16),
            pltpu.VMEM((8, 16, 128), jnp.bfloat16),
            pltpu.SemaphoreType.DMA((3,)),
        ],
        compiler_params=PARAMS,
    )(*[pltpu.with_memory_space_constraint(a, pltpu.HBM) for a in (right_side, near_bands, margins)])
    (answer,) = call(x_join, [(160, 128)], [])(exchange(sent, "row", ROWS, 1))
    y_solved, kept, sent = call(
        y_local, [(16, 9, 8, 128), (3, 36, 8, 128), (36, 128)], [(8, 128, 128), (36, 128)]
    )(x_solved, exchange(answer, "row", ROWS, 1), near_bands, margins)
    both = lax.all_gather(sent, "col", axis_index_groups=CORES, tiled=True)
    pair, sent = call(y_pair, [(36, 128), (288, 128)], [(36, 128)])(both)
    (update,) = call(y_join, [(VARS, 8, 16, 128)], [(VARS, 128, 128), (20, 8, 128)])(
        exchange(sent, "col", DEEP, 4), pair, y_solved, kept, near_bands, margins
    )
    return update


def solution(mesh):
    placed = (
        P(None, None, "row", "col"),
        P(None, None, None, "row", "col"),
        P(None, None, "row", "col"),
    )
    return jax.shard_map(
        body, mesh=mesh, in_specs=placed, out_specs=P(None, None, "row", "col"), check_vma=False
    )
```

```python
import jax
import jax.numpy as jnp
from jax import lax
from jax.experimental import pallas as pl
from jax.experimental.pallas import tpu as pltpu
from jax.sharding import PartitionSpec as P

VARS = 5
OUTER = 0.05
F32 = jnp.float32
PARAMS = pltpu.CompilerParams(vmem_limit_bytes=48 * 1024 * 1024)

HEAD, TAIL, HEAD_IN, TAIL_IN, HEAD_OUT, TAIL_OUT = 0, 10, 20, 24, 28, 32


def solve_block(below, middle, above, sources, cells):
    count = len(sources[0])
    ratio_one, ratio_two, reduced = [], [], []
    for i in range(cells):
        sub, mid, sup = below(i), middle(i), above(i)
        zero = jnp.zeros_like(mid)
        lower = sub + OUTER * ratio_one[i - 2] if i >= 2 else sub
        centre = mid + OUTER * ratio_two[i - 2] if i >= 2 else mid
        upper = sup
        if i >= 1:
            centre = centre - lower * ratio_one[i - 1]
            upper = sup - lower * ratio_two[i - 1]
        inverse = 1.0 / centre
        row = list(sources[i])
        row.append(zero - OUTER if i == 0 else zero)
        row.append(sub if i == 0 else zero - OUTER if i == 1 else zero)
        new = []
        for c in range(count + 2):
            value = row[c]
            if i >= 2:
                value = value + OUTER * reduced[i - 2][c]
            if i >= 1:
                value = value - lower * reduced[i - 1][c]
            new.append(value * inverse)
        if i == cells - 2:
            new += [-OUTER * inverse, zero]
        elif i == cells - 1:
            new += [(sup - lower * reduced[i - 1][count + 2]) * inverse, -OUTER * inverse]
        reduced.append(new)
        ratio_one.append(upper * inverse)
        ratio_two.append(-OUTER * inverse)
    solved = [None] * cells
    solved[cells - 1] = reduced[cells - 1]
    for i in range(cells - 2, -1, -1):
        out = []
        for c in range(count + 4):
            value = reduced[i][c] if c < len(reduced[i]) else None
            term = ratio_one[i] * solved[i + 1][c]
            value = -term if value is None else value - term
            if i + 2 < cells:
                value = value - ratio_two[i] * solved[i + 2][c]
            out.append(value)
        solved[i] = out
    return solved


def relation_of(solved):
    first, second, before, last = solved[0], solved[1], solved[-2], solved[-1]
    relation = []
    for pair in ((first, second), (before, last)):
        for cell in pair:
            relation += cell[:VARS]
    for lo in (VARS, VARS + 2):
        for pair in ((first, second), (before, last)):
            for cell in pair:
                relation += cell[lo : lo + 2]
    return relation


def product(left, right):
    wide = len(right) // 2
    return [
        left[2 * r] * right[c] + left[2 * r + 1] * right[wide + c] for r in range(2) for c in range(wide)
    ]


def plus(a, b):
    return [x + y for x, y in zip(a, b)]


def minus(a, b):
    return [x - y for x, y in zip(a, b)]


def parts(relation):
    return (
        relation[HEAD:TAIL],
        relation[TAIL:HEAD_IN],
        relation[HEAD_IN:TAIL_IN],
        relation[TAIL_IN:HEAD_OUT],
        relation[HEAD_OUT:TAIL_OUT],
        relation[TAIL_OUT:],
    )


def merge(left, right):
    hv_a, tv_a, hin_a, tin_a, hout_a, tout_a = parts(left)
    hv_b, tv_b, hin_b, tin_b, hout_b, tout_b = parts(right)
    loop = product(tout_a, hin_b)
    a, b, c, d = 1.0 - loop[0], -loop[1], -loop[2], 1.0 - loop[3]
    inverse = 1.0 / (a * d - b * c)
    shift = [d * inverse, -b * inverse, -c * inverse, a * inverse]
    jv = product(shift, minus(tv_a, product(tout_a, hv_b)))
    jp = product(shift, tin_a)
    jf = product(shift, product(tout_a, hout_b))
    kv = minus(hv_b, product(hin_b, jv))
    kp = product(hin_b, jp)
    kf = plus(product(hin_b, jf), hout_b)
    merged = (
        minus(hv_a, product(hout_a, kv))
        + minus(tv_b, product(tin_b, jv))
        + plus(hin_a, product(hout_a, kp))
        + [-x for x in product(tin_b, jp)]
        + [-x for x in product(hout_a, kf)]
        + plus(product(tin_b, jf), tout_b)
    )
    return merged, jv + kv + jp + jf + kp + kf


def joint(saved, prev, following):
    jv, kv, jp, jf, kp, kf = saved[:10], saved[10:20], saved[20:24], saved[24:28], saved[28:32], saved[32:]
    if prev is None:
        return jv, kv
    tail = plus(minus(jv, product(jp, prev)), product(jf, following))
    head = minus(plus(kv, product(kp, prev)), product(kf, following))
    return tail, head


def rolled(values, shift, axis):
    return [pltpu.roll(v, shift, axis) for v in values]


def climb(relation, levels):
    kept = []
    for axis, distance, size, mirrored in levels:
        other = rolled(relation, size - distance, axis)
        relation, saved = merge(other, relation) if mirrored else merge(relation, other)
        kept.append(saved)
    return relation, kept


def descend(kept, levels, prev, following):
    for saved, (axis, distance, size, mirrored) in zip(reversed(kept), reversed(levels)):
        tail, head = joint(saved, prev, following)
        place = lax.broadcasted_iota(jnp.int32, (8, 128), axis)
        far = (place & distance) != 0
        if prev is None:
            prev = following = [jnp.zeros((8, 128), F32)] * 10
        if mirrored:
            prev = [jnp.where(far, pltpu.roll(p, distance, axis), t) for t, p in zip(tail, prev)]
            following = [jnp.where(far, pltpu.roll(h, distance, axis), f) for f, h in zip(following, head)]
        else:
            prev = [jnp.where(far, pltpu.roll(t, distance, axis), p) for t, p in zip(tail, prev)]
            following = [jnp.where(far, pltpu.roll(f, distance, axis), h) for f, h in zip(following, head)]
    return prev, following


def swap_quarters(four):
    lane = lax.broadcasted_iota(jnp.int32, (8, 128), 1)
    low_two, low_one = (lane & 64) == 0, (lane & 32) == 0
    half = [None] * 4
    for j in (0, 1):
        a, b = four[j], four[j + 2]
        half[j] = jnp.where(low_two, a, pltpu.roll(b, 64, 1))
        half[j + 2] = jnp.where(low_two, pltpu.roll(a, 64, 1), b)
    out = [None] * 4
    for j in (0, 2):
        a, b = half[j], half[j + 1]
        out[j] = jnp.where(low_one, a, pltpu.roll(b, 32, 1))
        out[j + 1] = jnp.where(low_one, pltpu.roll(a, 96, 1), b)
    return out


ROW_MASK, DEEP_ORDER = 20, (6, 7, 5, 4, 3, 2, 1, 0)
ROWS = [[k ^ ROW_MASK for k in range(32)]]
DEEP = [[2 * z + core for z in DEEP_ORDER] for core in range(2)]
CORES = [[2 * z, 2 * z + 1] for z in range(8)]

SUB_LEVELS = tuple((0, 1 << bit, 8, False) for bit in range(3))
ROW_LEVELS = tuple((1, 32 << bit, 128, bool(ROW_MASK >> bit & 1)) for bit in range(2))
ROW_LEVELS += tuple((0, 1 << bit, 8, bool(ROW_MASK >> bit + 2 & 1)) for bit in range(3))


def bands_of(bands_ref, margins_ref, direction):
    below = bands_ref[direction, 0].astype(F32)
    above = bands_ref[direction, 1].astype(F32)
    middle = jnp.abs(below) + jnp.abs(above) + 0.1 + margins_ref[direction].astype(F32)
    return below, middle, above


def x_local(right_hbm, bands_hbm, margins_hbm, solved_ref, sent_ref, lines, right, bands, margins, arrived):
    copies = [
        pltpu.make_async_copy(bands_hbm.at[0], bands, arrived.at[0]),
        pltpu.make_async_copy(margins_hbm.at[0], margins, arrived.at[1]),
        pltpu.make_async_copy(right_hbm, right, arrived.at[2]),
    ]
    for copy in copies:
        copy.start()
    copies[0].wait()
    copies[1].wait()
    below, above = bands[0].astype(F32), bands[1].astype(F32)
    middle = jnp.abs(below) + jnp.abs(above) + 0.1 + margins[...].astype(F32)
    for slot, array in enumerate((below, middle, above)):
        lines[slot] = array.reshape(128, 128)
    copies[2].wait()
    for v in range(VARS):
        lines[3 + v] = right[v].astype(F32).reshape(128, 128)

    def cell(slot):
        return lambda i: lines[slot, pl.ds(i, 8, stride=16), :]

    sources = [[cell(3 + v)(i) for v in range(VARS)] for i in range(16)]
    solved = solve_block(cell(0), cell(1), cell(2), sources, 16)
    for i in range(16):
        for c in range(VARS + 4):
            solved_ref[i, c] = solved[i][c]
    relation = relation_of(solved)
    for g in range(9):
        out = swap_quarters(relation[4 * g : 4 * g + 4])
        for quarter in range(4):
            sent_ref[pl.ds(quarter * 9 + g, 8, stride=36), :] = out[quarter]


def send_to_all(relation, sent_ref, row, count):
    for c in range(36):
        row[c : c + 1, :] = relation[c][0:1, :]
    whole = row[...]
    for j in range(count):
        sent_ref[j * 36 : j * 36 + 36, :] = whole


def own_part(values, place, row):
    for c, value in enumerate(values):
        row[c] = value
    return [jnp.broadcast_to(row[c, pl.ds(place, 1), :], (8, 128)) for c in range(len(values))]


def x_join(got_ref, sent_ref):
    relation = []
    for g in range(9):
        relation += swap_quarters([got_ref[pl.ds(quarter * 9 + g, 8, stride=36), :] for quarter in range(4)])
    _, kept = climb(relation, ROW_LEVELS)
    prev, following = descend(kept, ROW_LEVELS, None, None)
    answer = prev + following
    for g in range(5):
        out = swap_quarters(answer[4 * g : 4 * g + 4])
        for quarter in range(4):
            sent_ref[pl.ds(quarter * 5 + g, 8, stride=20), :] = out[quarter]


def with_neighbours(cell, prev, following):
    before_one, before_two, after_one, after_two = cell[VARS:]
    return [
        cell[v]
        - before_one * prev[v]
        - before_two * prev[VARS + v]
        - after_one * following[v]
        - after_two * following[VARS + v]
        for v in range(VARS)
    ]


def y_local(x_solved_ref, got_ref, bands_ref, margins_ref, solved_ref, kept_ref, sent_ref, lines, row):
    answer = []
    for g in range(5):
        answer += swap_quarters([got_ref[pl.ds(quarter * 5 + g, 8, stride=20), :] for quarter in range(4)])
    prev, following = answer[:10], answer[10:]
    for i in range(16):
        cell = [x_solved_ref[i, c] for c in range(VARS + 4)]
        for v, value in enumerate(with_neighbours(cell, prev, following)):
            lines[3 + v, pl.ds(i, 8, stride=16), :] = value
    for slot, array in enumerate(bands_of(bands_ref, margins_ref, 1)):
        lines[slot] = array.reshape(128, 128).T
    for v in range(VARS):
        lines[3 + v] = lines[3 + v].T

    def cell_of(slot):
        return lambda i: lines[slot, pl.ds(i, 8, stride=16), :]

    sources = [[cell_of(3 + v)(i) for v in range(VARS)] for i in range(16)]
    solved = solve_block(cell_of(0), cell_of(1), cell_of(2), sources, 16)
    for i in range(16):
        for c in range(VARS + 4):
            solved_ref[i, c] = solved[i][c]
    relation, kept = climb(relation_of(solved), SUB_LEVELS)
    for level in range(3):
        for c in range(36):
            kept_ref[level, c] = kept[level][c]
    send_to_all(relation, sent_ref, row, 1)


def y_pair(got_ref, pair_ref, sent_ref, row):
    left, right = ([got_ref[36 * s + c : 36 * s + c + 1, :] for c in range(36)] for s in range(2))
    relation, pair = merge(left, right)
    for c in range(36):
        pair_ref[c : c + 1, :] = pair[c]
    send_to_all(relation, sent_ref, row, 8)


def y_join(got_ref, pair_ref, y_solved_ref, kept_ref, bands_ref, margins_ref, out_ref, lines, row, ordered):
    mine = lax.axis_index("col")
    for position, z in enumerate(DEEP_ORDER):
        ordered[z * 40 : z * 40 + 36, :] = got_ref[position * 36 : position * 36 + 36, :]
    _, kept = climb([ordered[pl.ds(c, 8, stride=40), :] for c in range(36)], SUB_LEVELS)
    prev, following = descend(kept, SUB_LEVELS, None, None)
    own = own_part(prev + following, mine // 2, row)
    prev, following = own[:10], own[10:]
    tail, head = joint([pair_ref[c : c + 1, :] for c in range(36)], prev, following)
    is_right = jnp.full((8, 128), mine % 2, jnp.int32) != 0
    own = [jnp.where(is_right, t, p) for t, p in zip(tail, prev)]
    own += [jnp.where(is_right, f, h) for f, h in zip(following, head)]
    kept = [[kept_ref[level, c] for c in range(36)] for level in range(3)]
    prev, following = descend(kept, SUB_LEVELS, own[:10], own[10:])
    for i in range(16):
        cell = [y_solved_ref[i, c] for c in range(VARS + 4)]
        for v, value in enumerate(with_neighbours(cell, prev, following)):
            lines[v, pl.ds(i, 8, stride=16), :] = value
    below, middle, above = bands_of(bands_ref, margins_ref, 2)
    ratio_one, ratio_two, reduced = [], [], []
    fields = [lines[v].T.reshape(8, 16, 128) for v in range(VARS)]
    for i in range(8):
        lower = below[i] + OUTER * ratio_one[i - 2] if i >= 2 else below[i]
        centre = middle[i] + OUTER * ratio_two[i - 2] if i >= 2 else middle[i]
        upper = above[i]
        if i >= 1:
            centre = centre - lower * ratio_one[i - 1]
            upper = upper - lower * ratio_two[i - 1]
        inverse = 1.0 / centre
        new = []
        for v in range(VARS):
            value = fields[v][i]
            if i >= 2:
                value = value + OUTER * reduced[i - 2][v]
            if i >= 1:
                value = value - lower * reduced[i - 1][v]
            new.append(value * inverse)
        reduced.append(new)
        ratio_one.append(upper * inverse)
        ratio_two.append(-OUTER * inverse)
    later = [None, None]
    for i in range(7, -1, -1):
        now = []
        for v in range(VARS):
            value = reduced[i][v]
            if later[0] is not None:
                value = value - ratio_one[i] * later[0][v]
            if later[1] is not None:
                value = value - ratio_two[i] * later[1][v]
            now.append(value)
            out_ref[v, i] = value
        later = [now, later[0]]


def call(kernel, outs, scratch):
    return pl.pallas_call(
        kernel,
        out_shape=[jax.ShapeDtypeStruct(shape, F32) for shape in outs],
        scratch_shapes=[pltpu.VMEM(shape, F32) for shape in scratch],
        compiler_params=PARAMS,
    )


def exchange(array, axis, members, rows):
    array = array.reshape(len(members[0]), -1, rows, 128)
    return lax.all_to_all(array, axis, 0, 0, tiled=True, axis_index_groups=members).reshape(-1, 128)


def body(right_side, near_bands, margins):
    x_solved, sent = pl.pallas_call(
        x_local,
        in_specs=[pl.BlockSpec(memory_space=pltpu.HBM)] * 3,
        out_shape=[jax.ShapeDtypeStruct((16, 9, 8, 128), F32), jax.ShapeDtypeStruct((288, 128), F32)],
        scratch_shapes=[
            pltpu.VMEM((8, 128, 128), F32),
            pltpu.VMEM((VARS, 8, 16, 128), jnp.bfloat16),
            pltpu.VMEM((2, 8, 16, 128), jnp.bfloat16),
            pltpu.VMEM((8, 16, 128), jnp.bfloat16),
            pltpu.SemaphoreType.DMA((3,)),
        ],
        compiler_params=PARAMS,
    )(*[pltpu.with_memory_space_constraint(a, pltpu.HBM) for a in (right_side, near_bands, margins)])
    (answer,) = call(x_join, [(160, 128)], [])(exchange(sent, "row", ROWS, 1))
    y_solved, kept, sent = call(
        y_local, [(16, 9, 8, 128), (3, 36, 8, 128), (36, 128)], [(8, 128, 128), (36, 128)]
    )(x_solved, exchange(answer, "row", ROWS, 1), near_bands, margins)
    both = lax.all_gather(sent, "col", axis_index_groups=CORES, tiled=True)
    pair, sent = call(y_pair, [(36, 128), (288, 128)], [(36, 128)])(both)
    (update,) = call(y_join, [(VARS, 8, 16, 128)], [(VARS, 128, 128), (20, 8, 128), (320, 128)])(
        exchange(sent, "col", DEEP, 4), pair, y_solved, kept, near_bands, margins
    )
    return update


def solution(mesh):
    placed = (
        P(None, None, "row", "col"),
        P(None, None, None, "row", "col"),
        P(None, None, "row", "col"),
    )
    return jax.shard_map(
        body, mesh=mesh, in_specs=placed, out_specs=P(None, None, "row", "col"), check_vma=False
    )
```

```python
import jax
import jax.numpy as jnp
from jax import lax
from jax.experimental import pallas as pl
from jax.experimental.pallas import tpu as pltpu
from jax.sharding import PartitionSpec as P

VARS = 5
OUTER = 0.05
PITCH = 24
F32 = jnp.float32
PARAMS = pltpu.CompilerParams(vmem_limit_bytes=48 * 1024 * 1024)

HEAD, TAIL, HEAD_IN, TAIL_IN, HEAD_OUT, TAIL_OUT = 0, 10, 20, 24, 28, 32


def solve_block(below, middle, above, sources, cells):
    count = len(sources[0])
    ratio_one, ratio_two, reduced = [], [], []
    for i in range(cells):
        sub, mid, sup = below(i), middle(i), above(i)
        zero = jnp.zeros_like(mid)
        lower = sub + OUTER * ratio_one[i - 2] if i >= 2 else sub
        centre = mid + OUTER * ratio_two[i - 2] if i >= 2 else mid
        upper = sup
        if i >= 1:
            centre = centre - lower * ratio_one[i - 1]
            upper = sup - lower * ratio_two[i - 1]
        inverse = 1.0 / centre
        row = list(sources[i])
        row.append(zero - OUTER if i == 0 else zero)
        row.append(sub if i == 0 else zero - OUTER if i == 1 else zero)
        new = []
        for c in range(count + 2):
            value = row[c]
            if i >= 2:
                value = value + OUTER * reduced[i - 2][c]
            if i >= 1:
                value = value - lower * reduced[i - 1][c]
            new.append(value * inverse)
        if i == cells - 2:
            new += [-OUTER * inverse, zero]
        elif i == cells - 1:
            new += [(sup - lower * reduced[i - 1][count + 2]) * inverse, -OUTER * inverse]
        reduced.append(new)
        ratio_one.append(upper * inverse)
        ratio_two.append(-OUTER * inverse)
    solved = [None] * cells
    solved[cells - 1] = reduced[cells - 1]
    for i in range(cells - 2, -1, -1):
        out = []
        for c in range(count + 4):
            value = reduced[i][c] if c < len(reduced[i]) else None
            term = ratio_one[i] * solved[i + 1][c]
            value = -term if value is None else value - term
            if i + 2 < cells:
                value = value - ratio_two[i] * solved[i + 2][c]
            out.append(value)
        solved[i] = out
    return solved


def relation_of(solved):
    first, second, before, last = solved[0], solved[1], solved[-2], solved[-1]
    relation = []
    for pair in ((first, second), (before, last)):
        for cell in pair:
            relation += cell[:VARS]
    for lo in (VARS, VARS + 2):
        for pair in ((first, second), (before, last)):
            for cell in pair:
                relation += cell[lo : lo + 2]
    return relation


def product(left, right):
    wide = len(right) // 2
    return [
        left[2 * r] * right[c] + left[2 * r + 1] * right[wide + c] for r in range(2) for c in range(wide)
    ]


def plus(a, b):
    return [x + y for x, y in zip(a, b)]


def minus(a, b):
    return [x - y for x, y in zip(a, b)]


def parts(relation):
    return (
        relation[HEAD:TAIL],
        relation[TAIL:HEAD_IN],
        relation[HEAD_IN:TAIL_IN],
        relation[TAIL_IN:HEAD_OUT],
        relation[HEAD_OUT:TAIL_OUT],
        relation[TAIL_OUT:],
    )


def merge(left, right):
    hv_a, tv_a, hin_a, tin_a, hout_a, tout_a = parts(left)
    hv_b, tv_b, hin_b, tin_b, hout_b, tout_b = parts(right)
    loop = product(tout_a, hin_b)
    a, b, c, d = 1.0 - loop[0], -loop[1], -loop[2], 1.0 - loop[3]
    inverse = 1.0 / (a * d - b * c)
    shift = [d * inverse, -b * inverse, -c * inverse, a * inverse]
    jv = product(shift, minus(tv_a, product(tout_a, hv_b)))
    jp = product(shift, tin_a)
    jf = product(shift, product(tout_a, hout_b))
    kv = minus(hv_b, product(hin_b, jv))
    kp = product(hin_b, jp)
    kf = plus(product(hin_b, jf), hout_b)
    merged = (
        minus(hv_a, product(hout_a, kv))
        + minus(tv_b, product(tin_b, jv))
        + plus(hin_a, product(hout_a, kp))
        + [-x for x in product(tin_b, jp)]
        + [-x for x in product(hout_a, kf)]
        + plus(product(tin_b, jf), tout_b)
    )
    return merged, jv + kv + jp + jf + kp + kf


def joint(saved, prev, following):
    jv, kv, jp, jf, kp, kf = saved[:10], saved[10:20], saved[20:24], saved[24:28], saved[28:32], saved[32:]
    if prev is None:
        return jv, kv
    tail = plus(minus(jv, product(jp, prev)), product(jf, following))
    head = minus(plus(kv, product(kp, prev)), product(kf, following))
    return tail, head


def rolled(values, shift, axis):
    return [pltpu.roll(v, shift, axis) for v in values]


def climb(relation, levels):
    kept = []
    for axis, distance, size, mirrored in levels:
        other = rolled(relation, size - distance, axis)
        relation, saved = merge(other, relation) if mirrored else merge(relation, other)
        kept.append(saved)
    return relation, kept


def descend(kept, levels, prev, following):
    for saved, (axis, distance, size, mirrored) in zip(reversed(kept), reversed(levels)):
        tail, head = joint(saved, prev, following)
        place = lax.broadcasted_iota(jnp.int32, (8, 128), axis)
        far = (place & distance) != 0
        if prev is None:
            prev = following = [jnp.zeros((8, 128), F32)] * 10
        if mirrored:
            prev = [jnp.where(far, pltpu.roll(p, distance, axis), t) for t, p in zip(tail, prev)]
            following = [jnp.where(far, pltpu.roll(h, distance, axis), f) for f, h in zip(following, head)]
        else:
            prev = [jnp.where(far, pltpu.roll(t, distance, axis), p) for t, p in zip(tail, prev)]
            following = [jnp.where(far, pltpu.roll(f, distance, axis), h) for f, h in zip(following, head)]
    return prev, following


def swap_quarters(four):
    lane = lax.broadcasted_iota(jnp.int32, (8, 128), 1)
    low_two, low_one = (lane & 64) == 0, (lane & 32) == 0
    half = [None] * 4
    for j in (0, 1):
        a, b = four[j], four[j + 2]
        half[j] = jnp.where(low_two, a, pltpu.roll(b, 64, 1))
        half[j + 2] = jnp.where(low_two, pltpu.roll(a, 64, 1), b)
    out = [None] * 4
    for j in (0, 2):
        a, b = half[j], half[j + 1]
        out[j] = jnp.where(low_one, a, pltpu.roll(b, 32, 1))
        out[j + 1] = jnp.where(low_one, pltpu.roll(a, 96, 1), b)
    return out


ROW_MASK, DEEP_ORDER = 20, (6, 7, 5, 4, 3, 2, 1, 0)
ROWS = [[k ^ ROW_MASK for k in range(32)]]
DEEP = [[2 * z + core for z in DEEP_ORDER] for core in range(2)]
CORES = [[2 * z, 2 * z + 1] for z in range(8)]

SUB_LEVELS = tuple((0, 1 << bit, 8, False) for bit in range(3))
ROW_LEVELS = tuple((1, 32 << bit, 128, bool(ROW_MASK >> bit & 1)) for bit in range(2))
ROW_LEVELS += tuple((0, 1 << bit, 8, bool(ROW_MASK >> bit + 2 & 1)) for bit in range(3))


def bands_of(bands_ref, margins_ref, direction):
    below = bands_ref[direction, 0].astype(F32)
    above = bands_ref[direction, 1].astype(F32)
    middle = jnp.abs(below) + jnp.abs(above) + 0.1 + margins_ref[direction].astype(F32)
    return below, middle, above


def put_pitched(lines, slot, array):
    for s in range(8):
        lines[slot, s * PITCH : s * PITCH + 16, :] = array[16 * s : 16 * s + 16, :]


def get_pitched(lines, slot):
    return jnp.concatenate([lines[slot, s * PITCH : s * PITCH + 16, :] for s in range(8)], axis=0)


def solve_pitched(lines):
    def cell(slot):
        return lambda i: lines[slot, pl.ds(i, 8, stride=PITCH), :]

    sources = [[cell(3 + v)(i) for v in range(VARS)] for i in range(16)]
    return solve_block(cell(0), cell(1), cell(2), sources, 16)


def x_local(right_hbm, bands_hbm, margins_hbm, solved_ref, sent_ref, lines, right, bands, margins, arrived):
    copies = [
        pltpu.make_async_copy(right_hbm, right, arrived.at[0]),
        pltpu.make_async_copy(bands_hbm.at[0], bands, arrived.at[1]),
        pltpu.make_async_copy(margins_hbm.at[0], margins, arrived.at[2]),
    ]
    for copy in copies:
        copy.start()
    copies[1].wait()
    copies[2].wait()
    below, above = bands[0].astype(F32), bands[1].astype(F32)
    middle = jnp.abs(below) + jnp.abs(above) + 0.1 + margins[...].astype(F32)
    for slot, array in enumerate((below, middle, above)):
        put_pitched(lines, slot, array.reshape(128, 128))
    copies[0].wait()
    for v in range(VARS):
        put_pitched(lines, 3 + v, right[v].astype(F32).reshape(128, 128))
    solved = solve_pitched(lines)
    for i in range(16):
        for c in range(VARS + 4):
            solved_ref[i, c] = solved[i][c]
    relation = relation_of(solved)
    for g in range(9):
        out = swap_quarters(relation[4 * g : 4 * g + 4])
        for quarter in range(4):
            sent_ref[pl.ds(quarter * 9 + g, 8, stride=36), :] = out[quarter]


def send_to_all(relation, sent_ref, row, count):
    for c in range(36):
        row[c : c + 1, :] = relation[c][0:1, :]
    whole = row[...]
    for j in range(count):
        sent_ref[j * 36 : j * 36 + 36, :] = whole


def own_part(values, place, row):
    for c, value in enumerate(values):
        row[c] = value
    return [jnp.broadcast_to(row[c, pl.ds(place, 1), :], (8, 128)) for c in range(len(values))]


def x_join(got_ref, sent_ref):
    relation = []
    for g in range(9):
        relation += swap_quarters([got_ref[pl.ds(quarter * 9 + g, 8, stride=36), :] for quarter in range(4)])
    _, kept = climb(relation, ROW_LEVELS)
    prev, following = descend(kept, ROW_LEVELS, None, None)
    answer = prev + following
    for g in range(5):
        out = swap_quarters(answer[4 * g : 4 * g + 4])
        for quarter in range(4):
            sent_ref[pl.ds(quarter * 5 + g, 8, stride=20), :] = out[quarter]


def with_neighbours(cell, prev, following):
    before_one, before_two, after_one, after_two = cell[VARS:]
    return [
        cell[v]
        - before_one * prev[v]
        - before_two * prev[VARS + v]
        - after_one * following[v]
        - after_two * following[VARS + v]
        for v in range(VARS)
    ]


def y_local(x_solved_ref, got_ref, bands_ref, margins_ref, solved_ref, kept_ref, sent_ref, lines, row):
    answer = []
    for g in range(5):
        answer += swap_quarters([got_ref[pl.ds(quarter * 5 + g, 8, stride=20), :] for quarter in range(4)])
    prev, following = answer[:10], answer[10:]
    for i in range(16):
        cell = [x_solved_ref[i, c] for c in range(VARS + 4)]
        for v, value in enumerate(with_neighbours(cell, prev, following)):
            lines[3 + v, pl.ds(i, 8, stride=PITCH), :] = value
    for slot, array in enumerate(bands_of(bands_ref, margins_ref, 1)):
        put_pitched(lines, slot, array.reshape(128, 128).T)
    for v in range(VARS):
        put_pitched(lines, 3 + v, get_pitched(lines, 3 + v).T)
    solved = solve_pitched(lines)
    for i in range(16):
        for c in range(VARS + 4):
            solved_ref[i, c] = solved[i][c]
    relation, kept = climb(relation_of(solved), SUB_LEVELS)
    for level in range(3):
        for c in range(36):
            kept_ref[level, c] = kept[level][c]
    send_to_all(relation, sent_ref, row, 1)


def y_pair(got_ref, pair_ref, sent_ref, row):
    left, right = ([got_ref[36 * s + c : 36 * s + c + 1, :] for c in range(36)] for s in range(2))
    relation, pair = merge(left, right)
    for c in range(36):
        pair_ref[c : c + 1, :] = pair[c]
    send_to_all(relation, sent_ref, row, 8)


def y_join(got_ref, pair_ref, y_solved_ref, kept_ref, bands_ref, margins_ref, out_ref, lines, row, ordered):
    mine = lax.axis_index("col")
    for position, z in enumerate(DEEP_ORDER):
        ordered[z * 40 : z * 40 + 36, :] = got_ref[position * 36 : position * 36 + 36, :]
    _, kept = climb([ordered[pl.ds(c, 8, stride=40), :] for c in range(36)], SUB_LEVELS)
    prev, following = descend(kept, SUB_LEVELS, None, None)
    own = own_part(prev + following, mine // 2, row)
    prev, following = own[:10], own[10:]
    tail, head = joint([pair_ref[c : c + 1, :] for c in range(36)], prev, following)
    is_right = jnp.full((8, 128), mine % 2, jnp.int32) != 0
    own = [jnp.where(is_right, t, p) for t, p in zip(tail, prev)]
    own += [jnp.where(is_right, f, h) for f, h in zip(following, head)]
    kept = [[kept_ref[level, c] for c in range(36)] for level in range(3)]
    prev, following = descend(kept, SUB_LEVELS, own[:10], own[10:])
    for i in range(16):
        cell = [y_solved_ref[i, c] for c in range(VARS + 4)]
        for v, value in enumerate(with_neighbours(cell, prev, following)):
            lines[v, pl.ds(i, 8, stride=PITCH), :] = value
    below, middle, above = bands_of(bands_ref, margins_ref, 2)
    ratio_one, ratio_two, reduced = [], [], []
    fields = [get_pitched(lines, v).T.reshape(8, 16, 128) for v in range(VARS)]
    for i in range(8):
        lower = below[i] + OUTER * ratio_one[i - 2] if i >= 2 else below[i]
        centre = middle[i] + OUTER * ratio_two[i - 2] if i >= 2 else middle[i]
        upper = above[i]
        if i >= 1:
            centre = centre - lower * ratio_one[i - 1]
            upper = upper - lower * ratio_two[i - 1]
        inverse = 1.0 / centre
        new = []
        for v in range(VARS):
            value = fields[v][i]
            if i >= 2:
                value = value + OUTER * reduced[i - 2][v]
            if i >= 1:
                value = value - lower * reduced[i - 1][v]
            new.append(value * inverse)
        reduced.append(new)
        ratio_one.append(upper * inverse)
        ratio_two.append(-OUTER * inverse)
    later = [None, None]
    for i in range(7, -1, -1):
        now = []
        for v in range(VARS):
            value = reduced[i][v]
            if later[0] is not None:
                value = value - ratio_one[i] * later[0][v]
            if later[1] is not None:
                value = value - ratio_two[i] * later[1][v]
            now.append(value)
            out_ref[v, i] = value
        later = [now, later[0]]


def call(kernel, outs, scratch):
    return pl.pallas_call(
        kernel,
        out_shape=[jax.ShapeDtypeStruct(shape, F32) for shape in outs],
        scratch_shapes=[pltpu.VMEM(shape, F32) for shape in scratch],
        compiler_params=PARAMS,
    )


def exchange(array, axis, members, rows):
    array = array.reshape(len(members[0]), -1, rows, 128)
    return lax.all_to_all(array, axis, 0, 0, tiled=True, axis_index_groups=members).reshape(-1, 128)


def body(right_side, near_bands, margins):
    x_solved, sent = pl.pallas_call(
        x_local,
        in_specs=[pl.BlockSpec(memory_space=pltpu.HBM)] * 3,
        out_shape=[jax.ShapeDtypeStruct((16, 9, 8, 128), F32), jax.ShapeDtypeStruct((288, 128), F32)],
        scratch_shapes=[
            pltpu.VMEM((8, 8 * PITCH, 128), F32),
            pltpu.VMEM((VARS, 8, 16, 128), jnp.bfloat16),
            pltpu.VMEM((2, 8, 16, 128), jnp.bfloat16),
            pltpu.VMEM((8, 16, 128), jnp.bfloat16),
            pltpu.SemaphoreType.DMA((3,)),
        ],
        compiler_params=PARAMS,
    )(*[pltpu.with_memory_space_constraint(a, pltpu.HBM) for a in (right_side, near_bands, margins)])
    (answer,) = call(x_join, [(160, 128)], [])(exchange(sent, "row", ROWS, 1))
    y_solved, kept, sent = call(
        y_local, [(16, 9, 8, 128), (3, 36, 8, 128), (36, 128)], [(8, 8 * PITCH, 128), (36, 128)]
    )(x_solved, exchange(answer, "row", ROWS, 1), near_bands, margins)
    both = lax.all_gather(sent, "col", axis_index_groups=CORES, tiled=True)
    pair, sent = call(y_pair, [(36, 128), (288, 128)], [(36, 128)])(both)
    (update,) = call(y_join, [(VARS, 8, 16, 128)], [(VARS, 8 * PITCH, 128), (20, 8, 128), (320, 128)])(
        exchange(sent, "col", DEEP, 4), pair, y_solved, kept, near_bands, margins
    )
    return update


def solution(mesh):
    placed = (
        P(None, None, "row", "col"),
        P(None, None, None, "row", "col"),
        P(None, None, "row", "col"),
    )
    return jax.shard_map(
        body, mesh=mesh, in_specs=placed, out_specs=P(None, None, "row", "col"), check_vma=False
    )
```

```python
import jax
import jax.numpy as jnp
from jax import lax
from jax.experimental import pallas as pl
from jax.experimental.pallas import tpu as pltpu
from jax.sharding import PartitionSpec as P

VARS = 5
OUTER = 0.05
PITCH = 24
F32 = jnp.float32
PARAMS = pltpu.CompilerParams(vmem_limit_bytes=48 * 1024 * 1024)

HEAD, TAIL, HEAD_IN, TAIL_IN, HEAD_OUT, TAIL_OUT = 0, 10, 20, 24, 28, 32


def solve_block(below, middle, above, sources, cells):
    count = len(sources[0])
    ratio_one, ratio_two, reduced = [], [], []
    for i in range(cells):
        sub, mid, sup = below(i), middle(i), above(i)
        zero = jnp.zeros_like(mid)
        lower = sub + OUTER * ratio_one[i - 2] if i >= 2 else sub
        centre = mid + OUTER * ratio_two[i - 2] if i >= 2 else mid
        upper = sup
        if i >= 1:
            centre = centre - lower * ratio_one[i - 1]
            upper = sup - lower * ratio_two[i - 1]
        inverse = 1.0 / centre
        row = list(sources[i])
        row.append(zero - OUTER if i == 0 else zero)
        row.append(sub if i == 0 else zero - OUTER if i == 1 else zero)
        new = []
        for c in range(count + 2):
            value = row[c]
            if i >= 2:
                value = value + OUTER * reduced[i - 2][c]
            if i >= 1:
                value = value - lower * reduced[i - 1][c]
            new.append(value * inverse)
        if i == cells - 2:
            new += [-OUTER * inverse, zero]
        elif i == cells - 1:
            new += [(sup - lower * reduced[i - 1][count + 2]) * inverse, -OUTER * inverse]
        reduced.append(new)
        ratio_one.append(upper * inverse)
        ratio_two.append(-OUTER * inverse)
    solved = [None] * cells
    solved[cells - 1] = reduced[cells - 1]
    for i in range(cells - 2, -1, -1):
        out = []
        for c in range(count + 4):
            value = reduced[i][c] if c < len(reduced[i]) else None
            term = ratio_one[i] * solved[i + 1][c]
            value = -term if value is None else value - term
            if i + 2 < cells:
                value = value - ratio_two[i] * solved[i + 2][c]
            out.append(value)
        solved[i] = out
    return solved


def relation_of(solved):
    first, second, before, last = solved[0], solved[1], solved[-2], solved[-1]
    relation = []
    for pair in ((first, second), (before, last)):
        for cell in pair:
            relation += cell[:VARS]
    for lo in (VARS, VARS + 2):
        for pair in ((first, second), (before, last)):
            for cell in pair:
                relation += cell[lo : lo + 2]
    return relation


def product(left, right):
    wide = len(right) // 2
    return [
        left[2 * r] * right[c] + left[2 * r + 1] * right[wide + c] for r in range(2) for c in range(wide)
    ]


def plus(a, b):
    return [x + y for x, y in zip(a, b)]


def minus(a, b):
    return [x - y for x, y in zip(a, b)]


def parts(relation):
    return (
        relation[HEAD:TAIL],
        relation[TAIL:HEAD_IN],
        relation[HEAD_IN:TAIL_IN],
        relation[TAIL_IN:HEAD_OUT],
        relation[HEAD_OUT:TAIL_OUT],
        relation[TAIL_OUT:],
    )


def merge(left, right):
    hv_a, tv_a, hin_a, tin_a, hout_a, tout_a = parts(left)
    hv_b, tv_b, hin_b, tin_b, hout_b, tout_b = parts(right)
    loop = product(tout_a, hin_b)
    a, b, c, d = 1.0 - loop[0], -loop[1], -loop[2], 1.0 - loop[3]
    inverse = 1.0 / (a * d - b * c)
    shift = [d * inverse, -b * inverse, -c * inverse, a * inverse]
    jv = product(shift, minus(tv_a, product(tout_a, hv_b)))
    jp = product(shift, tin_a)
    jf = product(shift, product(tout_a, hout_b))
    kv = minus(hv_b, product(hin_b, jv))
    kp = product(hin_b, jp)
    kf = plus(product(hin_b, jf), hout_b)
    merged = (
        minus(hv_a, product(hout_a, kv))
        + minus(tv_b, product(tin_b, jv))
        + plus(hin_a, product(hout_a, kp))
        + [-x for x in product(tin_b, jp)]
        + [-x for x in product(hout_a, kf)]
        + plus(product(tin_b, jf), tout_b)
    )
    return merged, jv + kv + jp + jf + kp + kf


def joint(saved, prev, following):
    jv, kv, jp, jf, kp, kf = saved[:10], saved[10:20], saved[20:24], saved[24:28], saved[28:32], saved[32:]
    if prev is None:
        return jv, kv
    tail = plus(minus(jv, product(jp, prev)), product(jf, following))
    head = minus(plus(kv, product(kp, prev)), product(kf, following))
    return tail, head


def rolled(values, shift, axis):
    return [pltpu.roll(v, shift, axis) for v in values]


def climb(relation, levels):
    kept = []
    for axis, distance, size, mirrored in levels:
        other = rolled(relation, size - distance, axis)
        relation, saved = merge(other, relation) if mirrored else merge(relation, other)
        kept.append(saved)
    return relation, kept


def descend(kept, levels, prev, following):
    for saved, (axis, distance, size, mirrored) in zip(reversed(kept), reversed(levels)):
        tail, head = joint(saved, prev, following)
        place = lax.broadcasted_iota(jnp.int32, (8, 128), axis)
        far = (place & distance) != 0
        if prev is None:
            prev = following = [jnp.zeros((8, 128), F32)] * 10
        if mirrored:
            prev = [jnp.where(far, pltpu.roll(p, distance, axis), t) for t, p in zip(tail, prev)]
            following = [jnp.where(far, pltpu.roll(h, distance, axis), f) for f, h in zip(following, head)]
        else:
            prev = [jnp.where(far, pltpu.roll(t, distance, axis), p) for t, p in zip(tail, prev)]
            following = [jnp.where(far, pltpu.roll(f, distance, axis), h) for f, h in zip(following, head)]
    return prev, following


def swap_quarters(four):
    lane = lax.broadcasted_iota(jnp.int32, (8, 128), 1)
    low_two, low_one = (lane & 64) == 0, (lane & 32) == 0
    half = [None] * 4
    for j in (0, 1):
        a, b = four[j], four[j + 2]
        half[j] = jnp.where(low_two, a, pltpu.roll(b, 64, 1))
        half[j + 2] = jnp.where(low_two, pltpu.roll(a, 64, 1), b)
    out = [None] * 4
    for j in (0, 2):
        a, b = half[j], half[j + 1]
        out[j] = jnp.where(low_one, a, pltpu.roll(b, 32, 1))
        out[j + 1] = jnp.where(low_one, pltpu.roll(a, 96, 1), b)
    return out


ROW_MASK, DEEP_ORDER = 20, (6, 7, 5, 4, 3, 2, 1, 0)
ROWS = [[k ^ ROW_MASK for k in range(32)]]
DEEP = [[2 * z + core for z in DEEP_ORDER] for core in range(2)]
CORES = [[2 * z, 2 * z + 1] for z in range(8)]

SUB_LEVELS = tuple((0, 1 << bit, 8, False) for bit in range(3))
ROW_LEVELS = tuple((1, 32 << bit, 128, bool(ROW_MASK >> bit & 1)) for bit in range(2))
ROW_LEVELS += tuple((0, 1 << bit, 8, bool(ROW_MASK >> bit + 2 & 1)) for bit in range(3))


def bands_of(bands_ref, margins_ref, direction):
    below = bands_ref[direction, 0].astype(F32)
    above = bands_ref[direction, 1].astype(F32)
    middle = jnp.abs(below) + jnp.abs(above) + 0.1 + margins_ref[direction].astype(F32)
    return below, middle, above


def put_pitched(lines, slot, array):
    for s in range(8):
        lines[slot, s * PITCH : s * PITCH + 16, :] = array[16 * s : 16 * s + 16, :]


def get_pitched(lines, slot):
    return jnp.concatenate([lines[slot, s * PITCH : s * PITCH + 16, :] for s in range(8)], axis=0)


def solve_pitched(lines):
    def cell(slot):
        return lambda i: lines[slot, pl.ds(i, 8, stride=PITCH), :]

    sources = [[cell(3 + v)(i) for v in range(VARS)] for i in range(16)]
    return solve_block(cell(0), cell(1), cell(2), sources, 16)


def x_local(right_hbm, bands_hbm, margins_hbm, solved_ref, sent_ref, lines, right, bands, margins, arrived):
    copies = [
        pltpu.make_async_copy(bands_hbm.at[0, 0], bands.at[0], arrived.at[0]),
        pltpu.make_async_copy(bands_hbm.at[0, 1], bands.at[1], arrived.at[1]),
        pltpu.make_async_copy(margins_hbm.at[0], margins, arrived.at[2]),
    ]
    copies += [pltpu.make_async_copy(right_hbm.at[v], right.at[v], arrived.at[3 + v]) for v in range(VARS)]
    for copy in copies:
        copy.start()
    for copy in copies[:3]:
        copy.wait()
    below, above = bands[0].astype(F32), bands[1].astype(F32)
    middle = jnp.abs(below) + jnp.abs(above) + 0.1 + margins[...].astype(F32)
    for slot, array in enumerate((below, middle, above)):
        put_pitched(lines, slot, array.reshape(128, 128))
    for copy in copies[3:]:
        copy.wait()
    for v in range(VARS):
        put_pitched(lines, 3 + v, right[v].astype(F32).reshape(128, 128))
    solved = solve_pitched(lines)
    for i in range(16):
        for c in range(VARS + 4):
            solved_ref[i, c] = solved[i][c]
    relation = relation_of(solved)
    for g in range(9):
        out = swap_quarters(relation[4 * g : 4 * g + 4])
        for quarter in range(4):
            sent_ref[pl.ds(quarter * 9 + g, 8, stride=36), :] = out[quarter]


def send_to_all(relation, sent_ref, row, count):
    for c in range(36):
        row[c : c + 1, :] = relation[c][0:1, :]
    whole = row[...]
    for j in range(count):
        sent_ref[j * 36 : j * 36 + 36, :] = whole


def own_part(values, place, row):
    for c, value in enumerate(values):
        row[c] = value
    return [jnp.broadcast_to(row[c, pl.ds(place, 1), :], (8, 128)) for c in range(len(values))]


def x_join(got_ref, sent_ref):
    relation = []
    for g in range(9):
        relation += swap_quarters([got_ref[pl.ds(quarter * 9 + g, 8, stride=36), :] for quarter in range(4)])
    _, kept = climb(relation, ROW_LEVELS)
    prev, following = descend(kept, ROW_LEVELS, None, None)
    answer = prev + following
    for g in range(5):
        out = swap_quarters(answer[4 * g : 4 * g + 4])
        for quarter in range(4):
            sent_ref[pl.ds(quarter * 5 + g, 8, stride=20), :] = out[quarter]


def with_neighbours(cell, prev, following):
    before_one, before_two, after_one, after_two = cell[VARS:]
    return [
        cell[v]
        - before_one * prev[v]
        - before_two * prev[VARS + v]
        - after_one * following[v]
        - after_two * following[VARS + v]
        for v in range(VARS)
    ]


def y_local(x_solved_ref, got_ref, bands_ref, margins_ref, solved_ref, kept_ref, sent_ref, lines, row):
    answer = []
    for g in range(5):
        answer += swap_quarters([got_ref[pl.ds(quarter * 5 + g, 8, stride=20), :] for quarter in range(4)])
    prev, following = answer[:10], answer[10:]
    for i in range(16):
        cell = [x_solved_ref[i, c] for c in range(VARS + 4)]
        for v, value in enumerate(with_neighbours(cell, prev, following)):
            lines[3 + v, pl.ds(i, 8, stride=PITCH), :] = value
    for slot, array in enumerate(bands_of(bands_ref, margins_ref, 1)):
        put_pitched(lines, slot, array.reshape(128, 128).T)
    for v in range(VARS):
        put_pitched(lines, 3 + v, get_pitched(lines, 3 + v).T)
    solved = solve_pitched(lines)
    for i in range(16):
        for c in range(VARS + 4):
            solved_ref[i, c] = solved[i][c]
    relation, kept = climb(relation_of(solved), SUB_LEVELS)
    for level in range(3):
        for c in range(36):
            kept_ref[level, c] = kept[level][c]
    send_to_all(relation, sent_ref, row, 1)


def y_pair(got_ref, pair_ref, sent_ref, row):
    left, right = ([got_ref[36 * s + c : 36 * s + c + 1, :] for c in range(36)] for s in range(2))
    relation, pair = merge(left, right)
    for c in range(36):
        pair_ref[c : c + 1, :] = pair[c]
    send_to_all(relation, sent_ref, row, 8)


def y_join(got_ref, pair_ref, y_solved_ref, kept_ref, bands_ref, margins_ref, out_hbm, lines, row, ordered, out, left):
    mine = lax.axis_index("col")
    for position, z in enumerate(DEEP_ORDER):
        ordered[z * 40 : z * 40 + 36, :] = got_ref[position * 36 : position * 36 + 36, :]
    _, kept = climb([ordered[pl.ds(c, 8, stride=40), :] for c in range(36)], SUB_LEVELS)
    prev, following = descend(kept, SUB_LEVELS, None, None)
    own = own_part(prev + following, mine // 2, row)
    prev, following = own[:10], own[10:]
    tail, head = joint([pair_ref[c : c + 1, :] for c in range(36)], prev, following)
    is_right = jnp.full((8, 128), mine % 2, jnp.int32) != 0
    own = [jnp.where(is_right, t, p) for t, p in zip(tail, prev)]
    own += [jnp.where(is_right, f, h) for f, h in zip(following, head)]
    kept = [[kept_ref[level, c] for c in range(36)] for level in range(3)]
    prev, following = descend(kept, SUB_LEVELS, own[:10], own[10:])
    for i in range(16):
        cell = [y_solved_ref[i, c] for c in range(VARS + 4)]
        for v, value in enumerate(with_neighbours(cell, prev, following)):
            lines[v, pl.ds(i, 8, stride=PITCH), :] = value
    below, middle, above = bands_of(bands_ref, margins_ref, 2)
    lowers, inverses, ratio_one, ratio_two = [], [], [], []
    for i in range(8):
        lower = below[i] + OUTER * ratio_one[i - 2] if i >= 2 else below[i]
        centre = middle[i] + OUTER * ratio_two[i - 2] if i >= 2 else middle[i]
        upper = above[i]
        if i >= 1:
            centre = centre - lower * ratio_one[i - 1]
            upper = upper - lower * ratio_two[i - 1]
        inverse = 1.0 / centre
        lowers.append(lower)
        inverses.append(inverse)
        ratio_one.append(upper * inverse)
        ratio_two.append(-OUTER * inverse)
    copies = []
    for v in range(VARS):
        field = get_pitched(lines, v).T.reshape(8, 16, 128)
        reduced = []
        for i in range(8):
            value = field[i]
            if i >= 2:
                value = value + OUTER * reduced[i - 2]
            if i >= 1:
                value = value - lowers[i] * reduced[i - 1]
            reduced.append(value * inverses[i])
        for i in range(7, -1, -1):
            if i < 7:
                reduced[i] = reduced[i] - ratio_one[i] * reduced[i + 1]
            if i < 6:
                reduced[i] = reduced[i] - ratio_two[i] * reduced[i + 2]
            out[v, i] = reduced[i]
        copies.append(pltpu.make_async_copy(out.at[v], out_hbm.at[v], left.at[v]))
        copies[v].start()
    for copy in copies:
        copy.wait()


def call(kernel, outs, scratch):
    return pl.pallas_call(
        kernel,
        out_shape=[jax.ShapeDtypeStruct(shape, F32) for shape in outs],
        scratch_shapes=[pltpu.VMEM(shape, F32) for shape in scratch],
        compiler_params=PARAMS,
    )


def exchange(array, axis, members, rows):
    array = array.reshape(len(members[0]), -1, rows, 128)
    return lax.all_to_all(array, axis, 0, 0, tiled=True, axis_index_groups=members).reshape(-1, 128)


def body(right_side, near_bands, margins):
    x_solved, sent = pl.pallas_call(
        x_local,
        in_specs=[pl.BlockSpec(memory_space=pltpu.HBM)] * 3,
        out_shape=[jax.ShapeDtypeStruct((16, 9, 8, 128), F32), jax.ShapeDtypeStruct((288, 128), F32)],
        scratch_shapes=[
            pltpu.VMEM((8, 8 * PITCH, 128), F32),
            pltpu.VMEM((VARS, 8, 16, 128), jnp.bfloat16),
            pltpu.VMEM((2, 8, 16, 128), jnp.bfloat16),
            pltpu.VMEM((8, 16, 128), jnp.bfloat16),
            pltpu.SemaphoreType.DMA((3 + VARS,)),
        ],
        compiler_params=PARAMS,
    )(*[pltpu.with_memory_space_constraint(a, pltpu.HBM) for a in (right_side, near_bands, margins)])
    (answer,) = call(x_join, [(160, 128)], [])(exchange(sent, "row", ROWS, 1))
    y_solved, kept, sent = call(
        y_local, [(16, 9, 8, 128), (3, 36, 8, 128), (36, 128)], [(8, 8 * PITCH, 128), (36, 128)]
    )(x_solved, exchange(answer, "row", ROWS, 1), near_bands, margins)
    both = lax.all_gather(sent, "col", axis_index_groups=CORES, tiled=True)
    pair, sent = call(y_pair, [(36, 128), (288, 128)], [(36, 128)])(both)
    return pl.pallas_call(
        y_join,
        out_specs=pl.BlockSpec(memory_space=pltpu.HBM),
        out_shape=jax.ShapeDtypeStruct((VARS, 8, 16, 128), F32),
        scratch_shapes=[
            pltpu.VMEM((VARS, 8 * PITCH, 128), F32),
            pltpu.VMEM((20, 8, 128), F32),
            pltpu.VMEM((320, 128), F32),
            pltpu.VMEM((VARS, 8, 16, 128), F32),
            pltpu.SemaphoreType.DMA((VARS,)),
        ],
        compiler_params=PARAMS,
    )(exchange(sent, "col", DEEP, 4), pair, y_solved, kept, near_bands, margins)


def solution(mesh):
    placed = (
        P(None, None, "row", "col"),
        P(None, None, None, "row", "col"),
        P(None, None, "row", "col"),
    )
    return jax.shard_map(
        body, mesh=mesh, in_specs=placed, out_specs=P(None, None, "row", "col"), check_vma=False
    )
```

```python
import jax
import jax.numpy as jnp
from jax import lax
from jax.experimental import pallas as pl
from jax.experimental.pallas import tpu as pltpu
from jax.sharding import PartitionSpec as P

VARS = 5
OUTER = 0.05
PITCH = 24
F32 = jnp.float32
PARAMS = pltpu.CompilerParams(vmem_limit_bytes=48 * 1024 * 1024)

HEAD, TAIL, HEAD_IN, TAIL_IN, HEAD_OUT, TAIL_OUT = 0, 10, 20, 24, 28, 32


def solve_block(below, middle, above, sources, cells):
    count = len(sources[0])
    ratio_one, ratio_two, reduced = [], [], []
    for i in range(cells):
        sub, mid, sup = below(i), middle(i), above(i)
        zero = jnp.zeros_like(mid)
        lower = sub + OUTER * ratio_one[i - 2] if i >= 2 else sub
        centre = mid + OUTER * ratio_two[i - 2] if i >= 2 else mid
        upper = sup
        if i >= 1:
            centre = centre - lower * ratio_one[i - 1]
            upper = sup - lower * ratio_two[i - 1]
        inverse = 1.0 / centre
        row = list(sources[i])
        row.append(zero - OUTER if i == 0 else zero)
        row.append(sub if i == 0 else zero - OUTER if i == 1 else zero)
        new = []
        for c in range(count + 2):
            value = row[c]
            if i >= 2:
                value = value + OUTER * reduced[i - 2][c]
            if i >= 1:
                value = value - lower * reduced[i - 1][c]
            new.append(value * inverse)
        if i == cells - 2:
            new += [-OUTER * inverse, zero]
        elif i == cells - 1:
            new += [(sup - lower * reduced[i - 1][count + 2]) * inverse, -OUTER * inverse]
        reduced.append(new)
        ratio_one.append(upper * inverse)
        ratio_two.append(-OUTER * inverse)
    solved = [None] * cells
    solved[cells - 1] = reduced[cells - 1]
    for i in range(cells - 2, -1, -1):
        out = []
        for c in range(count + 4):
            value = reduced[i][c] if c < len(reduced[i]) else None
            term = ratio_one[i] * solved[i + 1][c]
            value = -term if value is None else value - term
            if i + 2 < cells:
                value = value - ratio_two[i] * solved[i + 2][c]
            out.append(value)
        solved[i] = out
    return solved


def relation_of(solved):
    first, second, before, last = solved[0], solved[1], solved[-2], solved[-1]
    relation = []
    for pair in ((first, second), (before, last)):
        for cell in pair:
            relation += cell[:VARS]
    for lo in (VARS, VARS + 2):
        for pair in ((first, second), (before, last)):
            for cell in pair:
                relation += cell[lo : lo + 2]
    return relation


def product(left, right):
    wide = len(right) // 2
    return [
        left[2 * r] * right[c] + left[2 * r + 1] * right[wide + c] for r in range(2) for c in range(wide)
    ]


def plus(a, b):
    return [x + y for x, y in zip(a, b)]


def minus(a, b):
    return [x - y for x, y in zip(a, b)]


def parts(relation):
    return (
        relation[HEAD:TAIL],
        relation[TAIL:HEAD_IN],
        relation[HEAD_IN:TAIL_IN],
        relation[TAIL_IN:HEAD_OUT],
        relation[HEAD_OUT:TAIL_OUT],
        relation[TAIL_OUT:],
    )


def merge(left, right):
    hv_a, tv_a, hin_a, tin_a, hout_a, tout_a = parts(left)
    hv_b, tv_b, hin_b, tin_b, hout_b, tout_b = parts(right)
    loop = product(tout_a, hin_b)
    a, b, c, d = 1.0 - loop[0], -loop[1], -loop[2], 1.0 - loop[3]
    inverse = 1.0 / (a * d - b * c)
    shift = [d * inverse, -b * inverse, -c * inverse, a * inverse]
    jv = product(shift, minus(tv_a, product(tout_a, hv_b)))
    jp = product(shift, tin_a)
    jf = product(shift, product(tout_a, hout_b))
    kv = minus(hv_b, product(hin_b, jv))
    kp = product(hin_b, jp)
    kf = plus(product(hin_b, jf), hout_b)
    merged = (
        minus(hv_a, product(hout_a, kv))
        + minus(tv_b, product(tin_b, jv))
        + plus(hin_a, product(hout_a, kp))
        + [-x for x in product(tin_b, jp)]
        + [-x for x in product(hout_a, kf)]
        + plus(product(tin_b, jf), tout_b)
    )
    return merged, jv + kv + jp + jf + kp + kf


def joint(saved, prev, following):
    jv, kv, jp, jf, kp, kf = saved[:10], saved[10:20], saved[20:24], saved[24:28], saved[28:32], saved[32:]
    if prev is None:
        return jv, kv
    tail = plus(minus(jv, product(jp, prev)), product(jf, following))
    head = minus(plus(kv, product(kp, prev)), product(kf, following))
    return tail, head


def rolled(values, shift, axis):
    return [pltpu.roll(v, shift, axis) for v in values]


def climb(relation, levels):
    kept = []
    for axis, distance, size, mirrored in levels:
        other = rolled(relation, size - distance, axis)
        relation, saved = merge(other, relation) if mirrored else merge(relation, other)
        kept.append(saved)
    return relation, kept


def descend(kept, levels, prev, following):
    for saved, (axis, distance, size, mirrored) in zip(reversed(kept), reversed(levels)):
        tail, head = joint(saved, prev, following)
        place = lax.broadcasted_iota(jnp.int32, (8, 128), axis)
        far = (place & distance) != 0
        if prev is None:
            prev = following = [jnp.zeros((8, 128), F32)] * 10
        if mirrored:
            prev = [jnp.where(far, pltpu.roll(p, distance, axis), t) for t, p in zip(tail, prev)]
            following = [jnp.where(far, pltpu.roll(h, distance, axis), f) for f, h in zip(following, head)]
        else:
            prev = [jnp.where(far, pltpu.roll(t, distance, axis), p) for t, p in zip(tail, prev)]
            following = [jnp.where(far, pltpu.roll(f, distance, axis), h) for f, h in zip(following, head)]
    return prev, following


def swap_quarters(four):
    lane = lax.broadcasted_iota(jnp.int32, (8, 128), 1)
    low_two, low_one = (lane & 64) == 0, (lane & 32) == 0
    half = [None] * 4
    for j in (0, 1):
        a, b = four[j], four[j + 2]
        half[j] = jnp.where(low_two, a, pltpu.roll(b, 64, 1))
        half[j + 2] = jnp.where(low_two, pltpu.roll(a, 64, 1), b)
    out = [None] * 4
    for j in (0, 2):
        a, b = half[j], half[j + 1]
        out[j] = jnp.where(low_one, a, pltpu.roll(b, 32, 1))
        out[j + 1] = jnp.where(low_one, pltpu.roll(a, 96, 1), b)
    return out


ROW_MASK, DEEP_ORDERS = 20, ((6, 7, 5, 4, 3, 2, 1, 0), (6, 2, 3, 7, 5, 4, 1, 0))
ROWS = [[k ^ ROW_MASK for k in range(32)]]
DEEP = [[2 * z + core for z in DEEP_ORDERS[core]] for core in range(2)]
CORES = [[2 * z, 2 * z + 1] for z in range(8)]

SUB_LEVELS = tuple((0, 1 << bit, 8, False) for bit in range(3))
ROW_LEVELS = tuple((1, 32 << bit, 128, bool(ROW_MASK >> bit & 1)) for bit in range(2))
ROW_LEVELS += tuple((0, 1 << bit, 8, bool(ROW_MASK >> bit + 2 & 1)) for bit in range(3))


def bands_of(bands_ref, margins_ref, direction):
    below = bands_ref[direction, 0].astype(F32)
    above = bands_ref[direction, 1].astype(F32)
    middle = jnp.abs(below) + jnp.abs(above) + 0.1 + margins_ref[direction].astype(F32)
    return below, middle, above


def put_pitched(lines, slot, array):
    for s in range(8):
        lines[slot, s * PITCH : s * PITCH + 16, :] = array[16 * s : 16 * s + 16, :]


def get_pitched(lines, slot):
    return jnp.concatenate([lines[slot, s * PITCH : s * PITCH + 16, :] for s in range(8)], axis=0)


def solve_pitched(lines):
    def cell(slot):
        return lambda i: lines[slot, pl.ds(i, 8, stride=PITCH), :]

    sources = [[cell(3 + v)(i) for v in range(VARS)] for i in range(16)]
    return solve_block(cell(0), cell(1), cell(2), sources, 16)


def x_local(right_hbm, bands_hbm, margins_hbm, solved_ref, sent_ref, lines, right, bands, margins, arrived):
    copies = [
        pltpu.make_async_copy(right_hbm, right, arrived.at[0]),
        pltpu.make_async_copy(bands_hbm.at[0], bands, arrived.at[1]),
        pltpu.make_async_copy(margins_hbm.at[0], margins, arrived.at[2]),
    ]
    for copy in copies:
        copy.start()
    copies[1].wait()
    copies[2].wait()
    below, above = bands[0].astype(F32), bands[1].astype(F32)
    middle = jnp.abs(below) + jnp.abs(above) + 0.1 + margins[...].astype(F32)
    for slot, array in enumerate((below, middle, above)):
        put_pitched(lines, slot, array.reshape(128, 128))
    copies[0].wait()
    for v in range(VARS):
        put_pitched(lines, 3 + v, right[v].astype(F32).reshape(128, 128))
    solved = solve_pitched(lines)
    for i in range(16):
        for c in range(VARS + 4):
            solved_ref[i, c] = solved[i][c]
    relation = relation_of(solved)
    for g in range(9):
        out = swap_quarters(relation[4 * g : 4 * g + 4])
        for quarter in range(4):
            sent_ref[pl.ds(quarter * 9 + g, 8, stride=36), :] = out[quarter]


def send_to_all(relation, sent_ref, row, count):
    for c in range(36):
        row[c : c + 1, :] = relation[c][0:1, :]
    whole = row[...]
    for j in range(count):
        sent_ref[j * 36 : j * 36 + 36, :] = whole


def own_part(values, place, row):
    for c, value in enumerate(values):
        row[c] = value
    return [jnp.broadcast_to(row[c, pl.ds(place, 1), :], (8, 128)) for c in range(len(values))]


def x_join(got_ref, sent_ref):
    relation = []
    for g in range(9):
        relation += swap_quarters([got_ref[pl.ds(quarter * 9 + g, 8, stride=36), :] for quarter in range(4)])
    _, kept = climb(relation, ROW_LEVELS)
    prev, following = descend(kept, ROW_LEVELS, None, None)
    answer = prev + following
    for g in range(5):
        out = swap_quarters(answer[4 * g : 4 * g + 4])
        for quarter in range(4):
            sent_ref[pl.ds(quarter * 5 + g, 8, stride=20), :] = out[quarter]


def with_neighbours(cell, prev, following):
    before_one, before_two, after_one, after_two = cell[VARS:]
    return [
        cell[v]
        - before_one * prev[v]
        - before_two * prev[VARS + v]
        - after_one * following[v]
        - after_two * following[VARS + v]
        for v in range(VARS)
    ]


def y_local(x_solved_ref, got_ref, bands_ref, margins_ref, solved_ref, kept_ref, sent_ref, lines, row):
    answer = []
    for g in range(5):
        answer += swap_quarters([got_ref[pl.ds(quarter * 5 + g, 8, stride=20), :] for quarter in range(4)])
    prev, following = answer[:10], answer[10:]
    for i in range(16):
        cell = [x_solved_ref[i, c] for c in range(VARS + 4)]
        for v, value in enumerate(with_neighbours(cell, prev, following)):
            lines[3 + v, pl.ds(i, 8, stride=PITCH), :] = value
    for slot, array in enumerate(bands_of(bands_ref, margins_ref, 1)):
        put_pitched(lines, slot, array.reshape(128, 128).T)
    for v in range(VARS):
        put_pitched(lines, 3 + v, get_pitched(lines, 3 + v).T)
    solved = solve_pitched(lines)
    for i in range(16):
        for c in range(VARS + 4):
            solved_ref[i, c] = solved[i][c]
    relation, kept = climb(relation_of(solved), SUB_LEVELS)
    for level in range(3):
        for c in range(36):
            kept_ref[level, c] = kept[level][c]
    send_to_all(relation, sent_ref, row, 1)


def y_pair(got_ref, pair_ref, sent_ref, row):
    left, right = ([got_ref[36 * s + c : 36 * s + c + 1, :] for c in range(36)] for s in range(2))
    relation, pair = merge(left, right)
    for c in range(36):
        pair_ref[c : c + 1, :] = pair[c]
    send_to_all(relation, sent_ref, row, 8)


def y_join(got_ref, pair_ref, y_solved_ref, kept_ref, bands_ref, margins_ref, out_ref, lines, row, ordered):
    mine = lax.axis_index("col")
    for position, (z_zero, z_one) in enumerate(zip(*DEEP_ORDERS)):
        start = pl.multiple_of((z_zero + (z_one - z_zero) * (mine % 2)) * 40, 8)
        ordered[pl.ds(start, 36), :] = got_ref[position * 36 : position * 36 + 36, :]
    _, kept = climb([ordered[pl.ds(c, 8, stride=40), :] for c in range(36)], SUB_LEVELS)
    prev, following = descend(kept, SUB_LEVELS, None, None)
    own = own_part(prev + following, mine // 2, row)
    prev, following = own[:10], own[10:]
    tail, head = joint([pair_ref[c : c + 1, :] for c in range(36)], prev, following)
    is_right = jnp.full((8, 128), mine % 2, jnp.int32) != 0
    own = [jnp.where(is_right, t, p) for t, p in zip(tail, prev)]
    own += [jnp.where(is_right, f, h) for f, h in zip(following, head)]
    kept = [[kept_ref[level, c] for c in range(36)] for level in range(3)]
    prev, following = descend(kept, SUB_LEVELS, own[:10], own[10:])
    for i in range(16):
        cell = [y_solved_ref[i, c] for c in range(VARS + 4)]
        for v, value in enumerate(with_neighbours(cell, prev, following)):
            lines[v, pl.ds(i, 8, stride=PITCH), :] = value
    below, middle, above = bands_of(bands_ref, margins_ref, 2)
    ratio_one, ratio_two, reduced = [], [], []
    fields = [get_pitched(lines, v).T.reshape(8, 16, 128) for v in range(VARS)]
    for i in range(8):
        lower = below[i] + OUTER * ratio_one[i - 2] if i >= 2 else below[i]
        centre = middle[i] + OUTER * ratio_two[i - 2] if i >= 2 else middle[i]
        upper = above[i]
        if i >= 1:
            centre = centre - lower * ratio_one[i - 1]
            upper = upper - lower * ratio_two[i - 1]
        inverse = 1.0 / centre
        new = []
        for v in range(VARS):
            value = fields[v][i]
            if i >= 2:
                value = value + OUTER * reduced[i - 2][v]
            if i >= 1:
                value = value - lower * reduced[i - 1][v]
            new.append(value * inverse)
        reduced.append(new)
        ratio_one.append(upper * inverse)
        ratio_two.append(-OUTER * inverse)
    later = [None, None]
    for i in range(7, -1, -1):
        now = []
        for v in range(VARS):
            value = reduced[i][v]
            if later[0] is not None:
                value = value - ratio_one[i] * later[0][v]
            if later[1] is not None:
                value = value - ratio_two[i] * later[1][v]
            now.append(value)
            out_ref[v, i] = value
        later = [now, later[0]]


def call(kernel, outs, scratch):
    return pl.pallas_call(
        kernel,
        out_shape=[jax.ShapeDtypeStruct(shape, F32) for shape in outs],
        scratch_shapes=[pltpu.VMEM(shape, F32) for shape in scratch],
        compiler_params=PARAMS,
    )


def exchange(array, axis, members, rows):
    array = array.reshape(len(members[0]), -1, rows, 128)
    return lax.all_to_all(array, axis, 0, 0, tiled=True, axis_index_groups=members).reshape(-1, 128)


def body(right_side, near_bands, margins):
    x_solved, sent = pl.pallas_call(
        x_local,
        in_specs=[pl.BlockSpec(memory_space=pltpu.HBM)] * 3,
        out_shape=[jax.ShapeDtypeStruct((16, 9, 8, 128), F32), jax.ShapeDtypeStruct((288, 128), F32)],
        scratch_shapes=[
            pltpu.VMEM((8, 8 * PITCH, 128), F32),
            pltpu.VMEM((VARS, 8, 16, 128), jnp.bfloat16),
            pltpu.VMEM((2, 8, 16, 128), jnp.bfloat16),
            pltpu.VMEM((8, 16, 128), jnp.bfloat16),
            pltpu.SemaphoreType.DMA((3,)),
        ],
        compiler_params=PARAMS,
    )(*[pltpu.with_memory_space_constraint(a, pltpu.HBM) for a in (right_side, near_bands, margins)])
    (answer,) = call(x_join, [(160, 128)], [])(exchange(sent, "row", ROWS, 1))
    y_solved, kept, sent = call(
        y_local, [(16, 9, 8, 128), (3, 36, 8, 128), (36, 128)], [(8, 8 * PITCH, 128), (36, 128)]
    )(x_solved, exchange(answer, "row", ROWS, 1), near_bands, margins)
    both = lax.all_gather(sent, "col", axis_index_groups=CORES, tiled=True)
    pair, sent = call(y_pair, [(36, 128), (288, 128)], [(36, 128)])(both)
    (update,) = call(y_join, [(VARS, 8, 16, 128)], [(VARS, 8 * PITCH, 128), (20, 8, 128), (320, 128)])(
        exchange(sent, "col", DEEP, 4), pair, y_solved, kept, near_bands, margins
    )
    return update


def solution(mesh):
    placed = (
        P(None, None, "row", "col"),
        P(None, None, None, "row", "col"),
        P(None, None, "row", "col"),
    )
    return jax.shard_map(
        body, mesh=mesh, in_specs=placed, out_specs=P(None, None, "row", "col"), check_vma=False
    )
```

```python
import jax
import jax.numpy as jnp
from jax import lax
from jax.experimental import pallas as pl
from jax.experimental.pallas import tpu as pltpu
from jax.sharding import PartitionSpec as P

VARS = 5
OUTER = 0.05
PITCH = 24
F32 = jnp.float32
PARAMS = pltpu.CompilerParams(vmem_limit_bytes=48 * 1024 * 1024)

HEAD, TAIL, HEAD_IN, TAIL_IN, HEAD_OUT, TAIL_OUT = 0, 10, 20, 24, 28, 32


def solve_block(below, middle, above, sources, cells):
    count = len(sources[0])
    ratio_one, ratio_two, reduced = [], [], []
    for i in range(cells):
        sub, mid, sup = below(i), middle(i), above(i)
        zero = jnp.zeros_like(mid)
        lower = sub + OUTER * ratio_one[i - 2] if i >= 2 else sub
        centre = mid + OUTER * ratio_two[i - 2] if i >= 2 else mid
        upper = sup
        if i >= 1:
            centre = centre - lower * ratio_one[i - 1]
            upper = sup - lower * ratio_two[i - 1]
        inverse = 1.0 / centre
        row = list(sources[i])
        row.append(zero - OUTER if i == 0 else zero)
        row.append(sub if i == 0 else zero - OUTER if i == 1 else zero)
        new = []
        for c in range(count + 2):
            value = row[c]
            if i >= 2:
                value = value + OUTER * reduced[i - 2][c]
            if i >= 1:
                value = value - lower * reduced[i - 1][c]
            new.append(value * inverse)
        if i == cells - 2:
            new += [-OUTER * inverse, zero]
        elif i == cells - 1:
            new += [(sup - lower * reduced[i - 1][count + 2]) * inverse, -OUTER * inverse]
        reduced.append(new)
        ratio_one.append(upper * inverse)
        ratio_two.append(-OUTER * inverse)
    solved = [None] * cells
    solved[cells - 1] = reduced[cells - 1]
    for i in range(cells - 2, -1, -1):
        out = []
        for c in range(count + 4):
            value = reduced[i][c] if c < len(reduced[i]) else None
            term = ratio_one[i] * solved[i + 1][c]
            value = -term if value is None else value - term
            if i + 2 < cells:
                value = value - ratio_two[i] * solved[i + 2][c]
            out.append(value)
        solved[i] = out
    return solved


def relation_of(solved):
    first, second, before, last = solved[0], solved[1], solved[-2], solved[-1]
    relation = []
    for pair in ((first, second), (before, last)):
        for cell in pair:
            relation += cell[:VARS]
    for lo in (VARS, VARS + 2):
        for pair in ((first, second), (before, last)):
            for cell in pair:
                relation += cell[lo : lo + 2]
    return relation


def product(left, right):
    wide = len(right) // 2
    return [
        left[2 * r] * right[c] + left[2 * r + 1] * right[wide + c] for r in range(2) for c in range(wide)
    ]


def plus(a, b):
    return [x + y for x, y in zip(a, b)]


def minus(a, b):
    return [x - y for x, y in zip(a, b)]


def parts(relation):
    return (
        relation[HEAD:TAIL],
        relation[TAIL:HEAD_IN],
        relation[HEAD_IN:TAIL_IN],
        relation[TAIL_IN:HEAD_OUT],
        relation[HEAD_OUT:TAIL_OUT],
        relation[TAIL_OUT:],
    )


def merge(left, right):
    hv_a, tv_a, hin_a, tin_a, hout_a, tout_a = parts(left)
    hv_b, tv_b, hin_b, tin_b, hout_b, tout_b = parts(right)
    loop = product(tout_a, hin_b)
    a, b, c, d = 1.0 - loop[0], -loop[1], -loop[2], 1.0 - loop[3]
    inverse = 1.0 / (a * d - b * c)
    shift = [d * inverse, -b * inverse, -c * inverse, a * inverse]
    jv = product(shift, minus(tv_a, product(tout_a, hv_b)))
    jp = product(shift, tin_a)
    jf = product(shift, product(tout_a, hout_b))
    kv = minus(hv_b, product(hin_b, jv))
    kp = product(hin_b, jp)
    kf = plus(product(hin_b, jf), hout_b)
    merged = (
        minus(hv_a, product(hout_a, kv))
        + minus(tv_b, product(tin_b, jv))
        + plus(hin_a, product(hout_a, kp))
        + [-x for x in product(tin_b, jp)]
        + [-x for x in product(hout_a, kf)]
        + plus(product(tin_b, jf), tout_b)
    )
    return merged, jv + kv + jp + jf + kp + kf


def joint(saved, prev, following):
    jv, kv, jp, jf, kp, kf = saved[:10], saved[10:20], saved[20:24], saved[24:28], saved[28:32], saved[32:]
    if prev is None:
        return jv, kv
    tail = plus(minus(jv, product(jp, prev)), product(jf, following))
    head = minus(plus(kv, product(kp, prev)), product(kf, following))
    return tail, head


def rolled(values, shift, axis):
    return [pltpu.roll(v, shift, axis) for v in values]


def climb(relation, levels):
    kept = []
    for axis, distance, size, mirrored in levels:
        other = rolled(relation, size - distance, axis)
        relation, saved = merge(other, relation) if mirrored else merge(relation, other)
        kept.append(saved)
    return relation, kept


def descend(kept, levels, prev, following):
    for saved, (axis, distance, size, mirrored) in zip(reversed(kept), reversed(levels)):
        tail, head = joint(saved, prev, following)
        place = lax.broadcasted_iota(jnp.int32, (8, 128), axis)
        far = (place & distance) != 0
        if prev is None:
            prev = following = [jnp.zeros((8, 128), F32)] * 10
        if mirrored:
            prev = [jnp.where(far, pltpu.roll(p, distance, axis), t) for t, p in zip(tail, prev)]
            following = [jnp.where(far, pltpu.roll(h, distance, axis), f) for f, h in zip(following, head)]
        else:
            prev = [jnp.where(far, pltpu.roll(t, distance, axis), p) for t, p in zip(tail, prev)]
            following = [jnp.where(far, pltpu.roll(f, distance, axis), h) for f, h in zip(following, head)]
    return prev, following


def swap_quarters(four):
    lane = lax.broadcasted_iota(jnp.int32, (8, 128), 1)
    low_two, low_one = (lane & 64) == 0, (lane & 32) == 0
    half = [None] * 4
    for j in (0, 1):
        a, b = four[j], four[j + 2]
        half[j] = jnp.where(low_two, a, pltpu.roll(b, 64, 1))
        half[j + 2] = jnp.where(low_two, pltpu.roll(a, 64, 1), b)
    out = [None] * 4
    for j in (0, 2):
        a, b = half[j], half[j + 1]
        out[j] = jnp.where(low_one, a, pltpu.roll(b, 32, 1))
        out[j + 1] = jnp.where(low_one, pltpu.roll(a, 96, 1), b)
    return out


ROW_MASK, DEEP_ORDER = 20, (6, 7, 5, 4, 3, 2, 1, 0)
ROWS = [[k ^ ROW_MASK for k in range(32)]]
DEEP = [[2 * z + core for z in DEEP_ORDER] for core in range(2)]
CORES = [[2 * z, 2 * z + 1] for z in range(8)]

SUB_LEVELS = tuple((0, 1 << bit, 8, False) for bit in range(3))
ROW_LEVELS = tuple((1, 32 << bit, 128, bool(ROW_MASK >> bit & 1)) for bit in range(2))
ROW_LEVELS += tuple((0, 1 << bit, 8, bool(ROW_MASK >> bit + 2 & 1)) for bit in range(3))


def bands_of(bands_ref, margins_ref, direction):
    below = bands_ref[direction, 0].astype(F32)
    above = bands_ref[direction, 1].astype(F32)
    middle = jnp.abs(below) + jnp.abs(above) + 0.1 + margins_ref[direction].astype(F32)
    return below, middle, above


def put_pitched(lines, slot, array):
    for s in range(8):
        lines[slot, s * PITCH : s * PITCH + 16, :] = array[16 * s : 16 * s + 16, :]


def get_pitched(lines, slot):
    return jnp.concatenate([lines[slot, s * PITCH : s * PITCH + 16, :] for s in range(8)], axis=0)


def solve_pitched(lines):
    def cell(slot):
        return lambda i: lines[slot, pl.ds(i, 8, stride=PITCH), :]

    sources = [[cell(3 + v)(i) for v in range(VARS)] for i in range(16)]
    return solve_block(cell(0), cell(1), cell(2), sources, 16)


def x_local(right_hbm, bands_hbm, margins_hbm, solved_ref, sent_ref, lines, right, bands, margins, arrived):
    copies = [
        pltpu.make_async_copy(bands_hbm.at[0, 0], bands.at[0], arrived.at[0]),
        pltpu.make_async_copy(bands_hbm.at[0, 1], bands.at[1], arrived.at[1]),
        pltpu.make_async_copy(margins_hbm.at[0], margins, arrived.at[2]),
    ]
    copies += [pltpu.make_async_copy(right_hbm.at[v], right.at[v], arrived.at[3 + v]) for v in range(VARS)]
    for copy in copies:
        copy.start()
    for copy in copies[:3]:
        copy.wait()
    below, above = bands[0].astype(F32), bands[1].astype(F32)
    middle = jnp.abs(below) + jnp.abs(above) + 0.1 + margins[...].astype(F32)
    for slot, array in enumerate((below, middle, above)):
        put_pitched(lines, slot, array.reshape(128, 128))
    for copy in copies[3:]:
        copy.wait()
    for v in range(VARS):
        put_pitched(lines, 3 + v, right[v].astype(F32).reshape(128, 128))
    solved = solve_pitched(lines)
    for i in range(16):
        for c in range(VARS + 4):
            solved_ref[i, c] = solved[i][c]
    relation = relation_of(solved)
    for g in range(9):
        out = swap_quarters(relation[4 * g : 4 * g + 4])
        for quarter in range(4):
            sent_ref[pl.ds(quarter * 9 + g, 8, stride=36), :] = out[quarter]


def send_to_all(relation, sent_ref, row, count):
    for c in range(36):
        row[c : c + 1, :] = relation[c][0:1, :]
    whole = row[...]
    for j in range(count):
        sent_ref[j * 36 : j * 36 + 36, :] = whole


def own_part(values, place, row):
    for c, value in enumerate(values):
        row[c] = value
    return [jnp.broadcast_to(row[c, pl.ds(place, 1), :], (8, 128)) for c in range(len(values))]


def x_join(got_ref, sent_ref):
    relation = []
    for g in range(9):
        relation += swap_quarters([got_ref[pl.ds(quarter * 9 + g, 8, stride=36), :] for quarter in range(4)])
    _, kept = climb(relation, ROW_LEVELS)
    prev, following = descend(kept, ROW_LEVELS, None, None)
    answer = prev + following
    for g in range(5):
        out = swap_quarters(answer[4 * g : 4 * g + 4])
        for quarter in range(4):
            sent_ref[pl.ds(quarter * 5 + g, 8, stride=20), :] = out[quarter]


def with_neighbours(cell, prev, following):
    before_one, before_two, after_one, after_two = cell[VARS:]
    return [
        cell[v]
        - before_one * prev[v]
        - before_two * prev[VARS + v]
        - after_one * following[v]
        - after_two * following[VARS + v]
        for v in range(VARS)
    ]


def y_local(x_solved_ref, got_ref, bands_ref, margins_ref, solved_ref, kept_ref, sent_ref, lines, row):
    answer = []
    for g in range(5):
        answer += swap_quarters([got_ref[pl.ds(quarter * 5 + g, 8, stride=20), :] for quarter in range(4)])
    prev, following = answer[:10], answer[10:]
    for i in range(16):
        cell = [x_solved_ref[i, c] for c in range(VARS + 4)]
        for v, value in enumerate(with_neighbours(cell, prev, following)):
            lines[3 + v, pl.ds(i, 8, stride=PITCH), :] = value
    for slot, array in enumerate(bands_of(bands_ref, margins_ref, 1)):
        put_pitched(lines, slot, array.reshape(128, 128).T)
    for v in range(VARS):
        put_pitched(lines, 3 + v, get_pitched(lines, 3 + v).T)
    solved = solve_pitched(lines)
    for i in range(16):
        for c in range(VARS + 4):
            solved_ref[i, c] = solved[i][c]
    relation, kept = climb(relation_of(solved), SUB_LEVELS)
    for level in range(3):
        for c in range(36):
            kept_ref[level, c] = kept[level][c]
    send_to_all(relation, sent_ref, row, 1)


def y_pair(got_ref, pair_ref, sent_ref, row):
    left, right = ([got_ref[36 * s + c : 36 * s + c + 1, :] for c in range(36)] for s in range(2))
    relation, pair = merge(left, right)
    for c in range(36):
        pair_ref[c : c + 1, :] = pair[c]
    send_to_all(relation, sent_ref, row, 8)


def y_join(got_ref, pair_ref, y_solved_ref, kept_ref, bands_ref, margins_ref, out_ref, lines, row, ordered):
    mine = lax.axis_index("col")
    for position, z in enumerate(DEEP_ORDER):
        ordered[z * 40 : z * 40 + 36, :] = got_ref[position * 36 : position * 36 + 36, :]
    _, kept = climb([ordered[pl.ds(c, 8, stride=40), :] for c in range(36)], SUB_LEVELS)
    prev, following = descend(kept, SUB_LEVELS, None, None)
    own = own_part(prev + following, mine // 2, row)
    prev, following = own[:10], own[10:]
    tail, head = joint([pair_ref[c : c + 1, :] for c in range(36)], prev, following)
    is_right = jnp.full((8, 128), mine % 2, jnp.int32) != 0
    own = [jnp.where(is_right, t, p) for t, p in zip(tail, prev)]
    own += [jnp.where(is_right, f, h) for f, h in zip(following, head)]
    kept = [[kept_ref[level, c] for c in range(36)] for level in range(3)]
    prev, following = descend(kept, SUB_LEVELS, own[:10], own[10:])
    for i in range(16):
        cell = [y_solved_ref[i, c] for c in range(VARS + 4)]
        for v, value in enumerate(with_neighbours(cell, prev, following)):
            lines[v, pl.ds(i, 8, stride=PITCH), :] = value
    below, middle, above = bands_of(bands_ref, margins_ref, 2)
    ratio_one, ratio_two, reduced = [], [], []
    fields = [get_pitched(lines, v).T.reshape(8, 16, 128) for v in range(VARS)]
    for i in range(8):
        lower = below[i] + OUTER * ratio_one[i - 2] if i >= 2 else below[i]
        centre = middle[i] + OUTER * ratio_two[i - 2] if i >= 2 else middle[i]
        upper = above[i]
        if i >= 1:
            centre = centre - lower * ratio_one[i - 1]
            upper = upper - lower * ratio_two[i - 1]
        inverse = 1.0 / centre
        new = []
        for v in range(VARS):
            value = fields[v][i]
            if i >= 2:
                value = value + OUTER * reduced[i - 2][v]
            if i >= 1:
                value = value - lower * reduced[i - 1][v]
            new.append(value * inverse)
        reduced.append(new)
        ratio_one.append(upper * inverse)
        ratio_two.append(-OUTER * inverse)
    later = [None, None]
    for i in range(7, -1, -1):
        now = []
        for v in range(VARS):
            value = reduced[i][v]
            if later[0] is not None:
                value = value - ratio_one[i] * later[0][v]
            if later[1] is not None:
                value = value - ratio_two[i] * later[1][v]
            now.append(value)
            out_ref[v, i] = value
        later = [now, later[0]]


def call(kernel, outs, scratch):
    return pl.pallas_call(
        kernel,
        out_shape=[jax.ShapeDtypeStruct(shape, F32) for shape in outs],
        scratch_shapes=[pltpu.VMEM(shape, F32) for shape in scratch],
        compiler_params=PARAMS,
    )


def exchange(array, axis, members, rows):
    array = array.reshape(len(members[0]), -1, rows, 128)
    return lax.all_to_all(array, axis, 0, 0, tiled=True, axis_index_groups=members).reshape(-1, 128)


def body(right_side, near_bands, margins):
    x_solved, sent = pl.pallas_call(
        x_local,
        in_specs=[pl.BlockSpec(memory_space=pltpu.HBM)] * 3,
        out_shape=[jax.ShapeDtypeStruct((16, 9, 8, 128), F32), jax.ShapeDtypeStruct((288, 128), F32)],
        scratch_shapes=[
            pltpu.VMEM((8, 8 * PITCH, 128), F32),
            pltpu.VMEM((VARS, 8, 16, 128), jnp.bfloat16),
            pltpu.VMEM((2, 8, 16, 128), jnp.bfloat16),
            pltpu.VMEM((8, 16, 128), jnp.bfloat16),
            pltpu.SemaphoreType.DMA((3 + VARS,)),
        ],
        compiler_params=PARAMS,
    )(*[pltpu.with_memory_space_constraint(a, pltpu.HBM) for a in (right_side, near_bands, margins)])
    (answer,) = call(x_join, [(160, 128)], [])(exchange(sent, "row", ROWS, 1))
    y_solved, kept, sent = call(
        y_local, [(16, 9, 8, 128), (3, 36, 8, 128), (36, 128)], [(8, 8 * PITCH, 128), (36, 128)]
    )(x_solved, exchange(answer, "row", ROWS, 1), near_bands, margins)
    both = lax.all_gather(sent, "col", axis_index_groups=CORES, tiled=True)
    pair, sent = call(y_pair, [(36, 128), (288, 128)], [(36, 128)])(both)
    (update,) = call(y_join, [(VARS, 8, 16, 128)], [(VARS, 8 * PITCH, 128), (20, 8, 128), (320, 128)])(
        exchange(sent, "col", DEEP, 4), pair, y_solved, kept, near_bands, margins
    )
    return update


def solution(mesh):
    placed = (
        P(None, None, "row", "col"),
        P(None, None, None, "row", "col"),
        P(None, None, "row", "col"),
    )
    return jax.shard_map(
        body, mesh=mesh, in_specs=placed, out_specs=P(None, None, "row", "col"), check_vma=False
    )
```
